32 devices in a mesh: groups: 2 (over y), points: 4 (over z), centers: 4 (over x, core).
Axes of the slice: x: 2, y: 2, z: 4, core: 2. Of those that a mesh axis runs over, the one named last changes fastest.
Arguments:
- train_points: bfloat16 [8192, 512], P(('groups', 'points')), parts along dimension 0, may hold values from -6 to 6
- saved_preds: float32 [8192, 128], P(('groups', 'points')), parts along dimension 0, may hold values from -6 to 6
- targets: float32 [8192, 128], P(('groups', 'points')), parts along dimension 0, may hold values from -6 to 6
- huber_delta: float32 [256], P('groups'), parts along dimension 0, may hold values from 0.3 to 3
- center_pos: bfloat16 [16384, 512], P(('groups', 'points', 'centers')), parts along dimension 0, may hold values from -6 to 6
- coefficients: bfloat16 [16384, 128], P(('groups', 'points', 'centers')), parts along dimension 0, may hold values from -0.8984375 to 0.8984375
- spread: bfloat16 [16384], P(('groups', 'points', 'centers')), parts along dimension 0, may hold values from 0.5 to 2
Outputs:
- grad_centers: float32 [16384, 512], P(('groups', 'points', 'centers')), parts along dimension 0
- grad_coef: float32 [16384, 128], P(('groups', 'points', 'centers')), parts along dimension 0
The draws below stay inside these ranges and needn't reach their ends.
There are 2 independent parts, one for each index of `groups`. The reference program is written for one: setup_inputs(seed, part) draws one part's arguments, and reference() takes and returns one part's arrays. A program takes and returns all parts, laid end to end along the dimension named above; each array names one. Nothing has to cross between parts.
All inputs are finite; a program needn't handle non-finite values.
Results may differ from the reference program's by a relative error of at most 0.0003.
Values may be sent and summed in bfloat16 or wider, within the bound.
A program may use at most 64 MiB of HBM per device.

```python
import math
import jax
import jax.numpy as jnp
from jax import lax

DIN = 512
DOUT = 128
PTS_DEV = 1024
NPTS = 4096
NC = 8192
N_POINTS = 4


def block_scale(own_key, extent, split, low, largest):
    loudness = 1.0
    for dim, shards_of in split:
        steps = jax.random.uniform(jax.random.fold_in(jax.random.fold_in(own_key, 6), dim), (shards_of,), jnp.float32, low / len(split), largest / len(split))
        loudness = loudness * jnp.repeat(jnp.exp(steps), extent[dim] // shards_of).reshape((-1,) + (1,) * (len(extent) - 1 - dim))
    return loudness


def centred(stream_key, dims, scale, limit, shards=(), held_as=jnp.bfloat16):
    drawn = scale * jax.random.normal(stream_key, dims, jnp.float32)
    if shards:
        drawn = drawn * block_scale(stream_key, dims, shards, -0.22, 0.18)
    return jnp.clip(drawn, -limit, limit).astype(held_as)


def setup_inputs(seed: int = 0, part: int = 0) -> dict:
    splits = jax.random.split(jax.random.key(seed), 8)
    own_keys = jax.random.split(jax.random.fold_in(splits[7], part), 8)
    train_points = centred(own_keys[0], (NPTS, DIN), 1.0, 6.0, ((0, 4),))
    saved_preds = centred(own_keys[1], (NPTS, DOUT), 1.0, 6.0, ((0, 4),), jnp.float32)
    targets = centred(own_keys[2], (NPTS, DOUT), 1.0, 6.0, ((0, 4),), jnp.float32)
    huber_delta = jnp.clip(jnp.exp(jax.random.uniform(own_keys[3], (DOUT,), jnp.float32, math.log(0.3), math.log(3.0))), 0.3, 3.0)
    center_pos = centred(own_keys[4], (NC, DIN), 1.0, 6.0, ((0, 16),))
    coefficients = centred(own_keys[5], (NC, DOUT), 0.15, 0.8984375, ((0, 16),))
    spread = jnp.clip(jnp.exp(math.log(2.0) - 1.3862944 * jax.random.uniform(own_keys[6], (NC,), jnp.float32) ** block_scale(own_keys[6], (NC,), ((0, 16),), -0.2, 0.2)), 0.5, 2.0).astype(jnp.bfloat16)
    return dict(train_points=train_points, saved_preds=saved_preds, targets=targets, huber_delta=huber_delta, center_pos=center_pos, coefficients=coefficients, spread=spread)


def reference(train_points, saved_preds, targets, huber_delta, center_pos, coefficients, spread):
    in_width = train_points.shape[1]
    center_sq = lax.optimization_barrier(jnp.sum(jnp.square(center_pos.astype(jnp.float32)), axis=1))
    rates = spread.astype(jnp.float32)
    point_blocks = train_points.reshape(N_POINTS, PTS_DEV, DIN)
    saved_blocks = saved_preds.reshape(N_POINTS, PTS_DEV, DOUT)
    target_blocks = targets.reshape(N_POINTS, PTS_DEV, DOUT)

    def accumulate(totals, inputs):
        coef_acc, moment, row_totals = totals
        row_block, saved_blk, target_blk = inputs
        point_sq = lax.optimization_barrier(jnp.sum(jnp.square(row_block.astype(jnp.float32)), axis=1))
        cross = jnp.dot(row_block, center_pos.T, preferred_element_type=jnp.float32)
        dist = point_sq[:, None] + center_sq[None, :] - 2.0 * cross
        kernel = jnp.exp(-rates[None, :] * dist / in_width).astype(jnp.bfloat16)
        panel_pred = jnp.dot(kernel, coefficients, preferred_element_type=jnp.float32)
        residual = panel_pred + saved_blk - target_blk
        cotangent = (residual / jnp.sqrt(1.0 + jnp.square(residual / huber_delta[None, :]))).astype(jnp.bfloat16)
        coef_acc = coef_acc + jnp.dot(kernel.T, cotangent, preferred_element_type=jnp.float32)
        mixing = jnp.dot(cotangent, coefficients.T, preferred_element_type=jnp.float32)
        weights = (kernel.astype(jnp.float32) * mixing).astype(jnp.bfloat16)
        row_totals = row_totals + lax.optimization_barrier(jnp.sum(weights.astype(jnp.float32), axis=0))
        moment = moment + jnp.dot(weights.T, row_block, preferred_element_type=jnp.float32)
        return ((coef_acc, moment, row_totals), None)
    start = (jnp.zeros((NC, DOUT), jnp.float32), jnp.zeros((NC, DIN), jnp.float32), jnp.zeros((NC,), jnp.float32))
    (grad_coef, moment, row_totals), _ = lax.scan(accumulate, start, (point_blocks, saved_blocks, target_blocks))
    grad_centers = (2.0 * rates / in_width)[:, None] * (moment - row_totals[:, None] * center_pos.astype(jnp.float32))
    return (grad_centers, grad_coef)
```

```python
import jax
import jax.numpy as jnp
from jax import lax
from jax.sharding import PartitionSpec as P


def per_device(train_points, saved_preds, targets, huber_delta, center_pos, coefficients, spread):
    n_points, in_width = train_points.shape
    n_cen = lax.axis_size("centers")
    own_rows = n_points // n_cen
    both = ("points", "centers")
    points = lax.all_gather(train_points, "points", axis=0, tiled=True)
    rates = spread.astype(jnp.float32)
    center_sq = jnp.sum(jnp.square(center_pos.astype(jnp.float32)), axis=1)
    point_sq = jnp.sum(jnp.square(points.astype(jnp.float32)), axis=1)
    cross = lax.dot_general(
        points, center_pos, (((1,), (1,)), ((), ())), preferred_element_type=jnp.float32
    )
    dist = point_sq[:, None] + center_sq[None, :] - 2.0 * cross
    kernel = jnp.exp(-rates[None, :] * dist / in_width).astype(jnp.bfloat16)
    partial_pred = jnp.dot(kernel, coefficients, preferred_element_type=jnp.float32)
    pred = lax.psum_scatter(partial_pred, both, scatter_dimension=0, tiled=True)
    first = lax.axis_index("centers") * own_rows
    saved = lax.dynamic_slice_in_dim(saved_preds, first, own_rows)
    target = lax.dynamic_slice_in_dim(targets, first, own_rows)
    residual = pred + saved - target
    own_cot = (residual / jnp.sqrt(1.0 + jnp.square(residual / huber_delta[None, :]))).astype(
        jnp.bfloat16
    )
    cotangent = lax.all_gather(own_cot, both, axis=0, tiled=True)
    grad_coef = lax.dot_general(
        kernel, cotangent, (((0,), (0,)), ((), ())), preferred_element_type=jnp.float32
    )
    mixing = lax.dot_general(
        cotangent, coefficients, (((1,), (1,)), ((), ())), preferred_element_type=jnp.float32
    )
    weights = (kernel.astype(jnp.float32) * mixing).astype(jnp.bfloat16)
    totals = jnp.sum(weights.astype(jnp.float32), axis=0)
    moment = lax.dot_general(
        weights, points, (((0,), (0,)), ((), ())), preferred_element_type=jnp.float32
    )
    grad_centers = (2.0 * rates / in_width)[:, None] * (
        moment - totals[:, None] * center_pos.astype(jnp.float32)
    )
    return (grad_centers, grad_coef)


def solution(mesh):
    rows = P(("groups", "points"), None)
    owned = P(("groups", "points", "centers"), None)
    return jax.shard_map(
        per_device,
        mesh=mesh,
        in_specs=(rows, rows, rows, P("groups"), owned, owned, P(("groups", "points", "centers"))),
        out_specs=(owned, owned),
        check_vma=False,
    )
```

```python
import functools

import jax
import jax.numpy as jnp
from jax import lax
from jax.experimental import pallas as pl
from jax.experimental.pallas import tpu as pltpu
from jax.sharding import PartitionSpec as P

CORES = 2
SUBS = 2
MESH = pl.DeviceIdType.MESH
f32, bf16 = jnp.float32, jnp.bfloat16


def body(Z, C, train, saved, target, delta, rates, cen, coef, gcen, gcoef,
         pts, kt, pred, pc, px, psum, pz, cot, cm2, coeft, csq, nrate, tot, sv, tg,
         zs, zr, xs, xr, cs, cr, pcs, pcr, pxs, pxr, pzs, pzr,
         czs, czr, cxs, cxr, ccs, ccr, ls):
    X = C // CORES
    q, width = pts.shape[2], pts.shape[3]
    sub = q // SUBS
    z, c = lax.axis_index("points"), lax.axis_index("centers")
    x, core = lax.div(c, CORES), lax.rem(c, CORES)
    other = 1 - core
    mate = x * CORES + other
    off = [lax.rem(x + k, X) for k in range(X)]
    back = [lax.rem(x + X - k, X) for k in range(X)]

    def remote(src, dst, ssem, rsem, **to):
        return pltpu.make_async_remote_copy(
            src_ref=src, dst_ref=dst, send_sem=ssem, recv_sem=rsem, device_id=to,
            device_id_type=MESH)

    def lane(xi, co):
        return xi * CORES + co

    def zcopy(way, b, s, own=False):
        rows = pl.ds(s * sub, sub)
        dst = pts.at[b, c, rows]
        src = train.at[c, rows] if own else dst
        to = z + 1 if way == 0 else z - 1
        return remote(src, dst, zs.at[way, b, s], zr.at[b, s], points=to)

    def xcopy(b, k, s, coming=False):
        li = lane(back[k], core) if coming else c
        ref = pts.at[b, li, pl.ds(s * sub, sub)]
        return remote(ref, ref, xs.at[b, k, s], xr.at[b, k, s], centers=lane(off[k], core))

    def ccopy(b, xi, s, coming=False):
        ref = pts.at[b, lane(xi, other if coming else core), pl.ds(s * sub, sub)]
        return remote(ref, ref, cs.at[b, xi, s], cr.at[b, xi, s], centers=mate)

    def pccopy(b):
        return remote(pred.at[b, other], pc.at[b], pcs.at[b], pcr.at[b], centers=mate)

    def pxcopy(b, k):
        return remote(pred.at[b, core, off[k]], px.at[b, k], pxs.at[b, k], pxr.at[b, k],
                      centers=lane(off[k], core))

    def pzcopy(b, src_z):
        return remote(psum.at[b], pz.at[src_z], pzs.at[b], pzr.at[src_z], points=b)

    def czcopy(b, to):
        ref = cot.at[b, core, x]
        return remote(ref, ref, czs.at[to], czr.at[b], points=to)

    def cxcopy(b, k, coming=False):
        ref = cot.at[b, core, back[k] if coming else x]
        return remote(ref, ref, cxs.at[b, k], cxr.at[b, k], centers=lane(off[k], core))

    def cccopy(b, xi, coming=False):
        ref = cot.at[b, other if coming else core, xi]
        return remote(ref, ref, ccs.at[b, xi], ccr.at[b, xi], centers=mate)

    def blocks(d, f, first=1):
        @pl.when((d >= first) & (d < Z) & (z - d >= 0))
        def _():
            f(z - d)

        @pl.when((d >= max(first, 1)) & (d < Z) & (z + d < Z))
        def _():
            f(z + d)

    barrier = pltpu.get_barrier_semaphore()
    for k in range(1, Z):
        pl.semaphore_signal(barrier, inc=1, device_id={"points": lax.rem(z + k, Z)},
                            device_id_type=MESH)
    for k in range(1, X):
        pl.semaphore_signal(barrier, inc=1, device_id={"centers": lane(off[k], core)},
                            device_id_type=MESH)
    pl.semaphore_signal(barrier, inc=1, device_id={"centers": mate}, device_id_type=MESH)
    own_points = pltpu.make_async_copy(train, pts.at[z], ls.at[0])
    own_saved = pltpu.make_async_copy(saved.at[c], sv, ls.at[1])
    own_target = pltpu.make_async_copy(target.at[c], tg, ls.at[2])
    own_points.start()
    own_saved.start()
    own_target.start()
    pl.semaphore_wait(barrier, Z - 1 + X - 1 + 1)

    for s in range(SUBS):
        @pl.when(z + 1 < Z)
        def _():
            zcopy(0, z, s, own=True).start()

        @pl.when(z > 0)
        def _():
            zcopy(1, z, s, own=True).start()

    n_cen = cen.shape[0]
    cen32 = cen[...].astype(f32)
    cm2[...] = (-2.0 * cen32).astype(bf16)
    coeft[...] = coef[...].astype(f32).T.astype(bf16)
    csq[...] = jnp.broadcast_to(jnp.sum(cen32 * cen32, axis=1, keepdims=True), (n_cen, 128))
    nrate[...] = jnp.broadcast_to(rates[...] * (-1.0 / width), (128, n_cen)).T
    gcen[...] = jnp.zeros_like(gcen)
    gcoef[...] = jnp.zeros_like(gcoef)
    tot[...] = jnp.zeros_like(tot)

    def wide(col):
        return jnp.concatenate([col] * (q // 128), axis=1)

    def forward(b):
        def piece(t, carry):
            rows_t = pts[b, t].T
            r32 = rows_t.astype(f32)
            psq = jnp.sum(r32 * r32, axis=0, keepdims=True)
            cross = jnp.dot(cm2[...], rows_t, preferred_element_type=f32)
            dist = (psq + wide(csq[...])) + cross
            k = jnp.exp(wide(nrate[...]) * dist).astype(bf16)
            kt[b, t] = k
            pred[b, lax.rem(t, CORES), lax.div(t, CORES)] = jnp.dot(
                coeft[...], k, preferred_element_type=f32)
            return carry
        lax.fori_loop(0, C, piece, 0)

    def backward(b):
        def piece(t, carry):
            ct = cot[b, lax.rem(t, CORES), lax.div(t, CORES)]
            k = kt[b, t]
            mix = lax.dot_general(coef[...], ct, (((1,), (1,)), ((), ())),
                                  preferred_element_type=f32)
            w = (k.astype(f32) * mix).astype(bf16)
            w32 = w.astype(f32)
            part = w32[:, :128]
            for i in range(1, q // 128):
                part = part + w32[:, i * 128:(i + 1) * 128]
            tot[...] += part
            gcen[...] += jnp.dot(w, pts[b, t], preferred_element_type=f32)
            gcoef[...] += jnp.dot(k, ct, preferred_element_type=f32)
            return carry
        lax.fori_loop(0, C, piece, 0)

    def arrive(b, s):
        zcopy(0, b, s).wait_recv()

        @pl.when((b < z) & (z + 1 < Z))
        def _():
            zcopy(0, b, s).start()

        @pl.when((b > z) & (z > 0))
        def _():
            zcopy(1, b, s).start()
        for k in range(1, X):
            xcopy(b, k, s).start()
        ccopy(b, x, s).start()

    def cross_x(b):
        for s in range(SUBS):
            for k in range(1, X):
                xcopy(b, k, s, coming=True).wait_recv()
                ccopy(b, back[k], s).start()

    def add_core(b):
        pccopy(b).wait_recv()
        pred[b, core] += pc[b]
        for k in range(1, X):
            pxcopy(b, k).start()

    def add_plane(b):
        total = pred[b, core, x]
        for k in range(1, X):
            pxcopy(b, k).wait_recv()
            total = total + px[b, k]
        psum[b] = total

        @pl.when(b != z)
        def _():
            pzcopy(b, z).start()

    def work(b):
        for xi in range(X):
            for s in range(SUBS):
                ccopy(b, xi, s, coming=True).wait_recv()
        forward(b)
        pccopy(b).start()

    own_points.wait()
    forward(z)
    pccopy(z).start()

    def step(d, carry):
        for s in range(SUBS):
            blocks(d, lambda b: arrive(b, s))
        blocks(d - 1, add_core, 0)
        blocks(d, cross_x)
        blocks(d - 1, add_plane, 0)
        blocks(d, work)
        return carry
    lax.fori_loop(1, Z + 1, step, 0)

    total = psum[z]
    for k in range(1, Z):
        src = lax.rem(z + k, Z)
        pzcopy(src, src).wait_recv()
        total = total + pz[src]
    own_saved.wait()
    own_target.wait()
    residual = total.T + sv[...] - tg[...]
    ratio = residual / delta[...]
    cot[z, core, x] = (residual / jnp.sqrt(1.0 + ratio * ratio)).astype(bf16)
    for k in range(1, Z):
        czcopy(z, lax.rem(z + k, Z)).start()

    def spread_cot(b):
        for k in range(1, X):
            cxcopy(b, k).start()
        cccopy(b, x).start()

    def cot_arrive(b):
        czcopy(b, b).wait_recv()
        spread_cot(b)

    def cot_work(b):
        for k in range(1, X):
            cxcopy(b, k, coming=True).wait_recv()
            cccopy(b, back[k]).start()
        for xi in range(X):
            cccopy(b, xi, coming=True).wait_recv()
        backward(b)

    spread_cot(z)

    def cot_step(d, carry):
        blocks(d, cot_arrive)
        blocks(d - 1, cot_work, 0)
        return carry
    lax.fori_loop(1, Z + 1, cot_step, 0)

    row_totals = jnp.sum(tot[...], axis=1, keepdims=True)
    scale = -2.0 * nrate[...]
    scale = jnp.concatenate([scale] * (width // 128), axis=1)
    gcen[...] = scale * (gcen[...] - row_totals * cen[...].astype(f32))

    def drain(b, carry):
        for s in range(SUBS):
            @pl.when((b <= z) & (z + 1 < Z))
            def _():
                zcopy(0, b, s).wait_send()

            @pl.when((b >= z) & (z > 0))
            def _():
                zcopy(1, b, s).wait_send()

        @pl.when(b != z)
        def _():
            for s in range(SUBS):
                for k in range(1, X):
                    xcopy(b, k, s).wait_send()
                for xi in range(X):
                    ccopy(b, xi, s).wait_send()
            pzcopy(b, z).wait_send()
            czcopy(z, b).wait_send()
        pccopy(b).wait_send()
        for k in range(1, X):
            pxcopy(b, k).wait_send()
            cxcopy(b, k).wait_send()
        for xi in range(X):
            cccopy(b, xi).wait_send()
        return carry
    lax.fori_loop(0, Z, drain, 0)


def per_device(Z, C, train_points, saved_preds, targets, huber_delta, center_pos, coefficients, spread):
    n_points, width = train_points.shape
    n_cen, n_out = coefficients.shape
    X, q = C // CORES, n_points // C
    vm, anywhere = pl.BlockSpec(memory_space=pltpu.VMEM), pl.BlockSpec(memory_space=pl.ANY)
    dma = pltpu.SemaphoreType.DMA
    flops = 2 * Z * n_points * n_cen * (2 * width + 3 * n_out)
    return tuple(pl.pallas_call(
        functools.partial(body, Z, C),
        out_shape=(jax.ShapeDtypeStruct((n_cen, width), f32),
                   jax.ShapeDtypeStruct((n_cen, n_out), f32)),
        in_specs=[anywhere] * 3 + [vm] * 4,
        out_specs=(vm, vm),
        scratch_shapes=[
            pltpu.VMEM((Z, C, q, width), bf16),
            pltpu.VMEM((Z, C, n_cen, q), bf16),
            pltpu.VMEM((Z, CORES, X, n_out, q), f32),
            pltpu.VMEM((Z, X, n_out, q), f32),
            pltpu.VMEM((Z, X, n_out, q), f32),
            pltpu.VMEM((Z, n_out, q), f32),
            pltpu.VMEM((Z, n_out, q), f32),
            pltpu.VMEM((Z, CORES, X, q, n_out), bf16),
            pltpu.VMEM((n_cen, width), bf16),
            pltpu.VMEM((n_out, n_cen), bf16),
            pltpu.VMEM((n_cen, 128), f32),
            pltpu.VMEM((n_cen, 128), f32),
            pltpu.VMEM((n_cen, 128), f32),
            pltpu.VMEM((q, n_out), f32),
            pltpu.VMEM((q, n_out), f32),
            dma((2, Z, SUBS)), dma((Z, SUBS)),
            dma((Z, X, SUBS)), dma((Z, X, SUBS)),
            dma((Z, X, SUBS)), dma((Z, X, SUBS)),
            dma((Z,)), dma((Z,)),
            dma((Z, X)), dma((Z, X)),
            dma((Z,)), dma((Z,)),
            dma((Z,)), dma((Z,)),
            dma((Z, X)), dma((Z, X)),
            dma((Z, X)), dma((Z, X)),
            dma((3,)),
        ],
        compiler_params=pltpu.CompilerParams(
            collective_id=0, has_side_effects=True, vmem_limit_bytes=60 << 20),
        cost_estimate=pl.CostEstimate(
            flops=flops, bytes_accessed=4 << 20, transcendentals=Z * n_points * n_cen),
    )(train_points.reshape(C, q, width), saved_preds.reshape(C, q, n_out),
      targets.reshape(C, q, n_out), huber_delta.reshape(1, n_out),
      spread.astype(f32).reshape(1, n_cen), center_pos, coefficients))


def solution(mesh):
    rows = P(("groups", "points"), None)
    owned = P(("groups", "points", "centers"), None)
    return jax.shard_map(
        functools.partial(per_device, mesh.shape["points"], mesh.shape["centers"]),
        mesh=mesh,
        in_specs=(rows, rows, rows, P("groups"), owned, owned, P(("groups", "points", "centers"))),
        out_specs=(owned, owned),
        check_vma=False,
    )
```

```python
import functools

import jax
import jax.numpy as jnp
from jax import lax
from jax.experimental import pallas as pl
from jax.experimental.pallas import tpu as pltpu
from jax.sharding import PartitionSpec as P

CORES = 2
SUBS = 2
LOG2E = 1.4426950408889634
MESH = pl.DeviceIdType.MESH
f32, bf16 = jnp.float32, jnp.bfloat16


def body(Z, C, train, saved, target, delta, rates, cen, coef, gcen, gcoef,
         pts, kt, pred, pc, px, psum, pz, cot, cm2, coeft, csq, nrate, tot, wbuf, sv, tg,
         zs, zr, xs, xr, cs, cr, pcs, pcr, pxs, pxr, pzs, pzr,
         czs, czr, cxs, cxr, ccs, ccr, ls):
    X = C // CORES
    q, width = pts.shape[2], pts.shape[3]
    sub = q // SUBS
    z, c = lax.axis_index("points"), lax.axis_index("centers")
    x, core = lax.div(c, CORES), lax.rem(c, CORES)
    other = 1 - core
    mate = x * CORES + other
    off = [lax.rem(x + k, X) for k in range(X)]
    back = [lax.rem(x + X - k, X) for k in range(X)]

    def remote(src, dst, ssem, rsem, **to):
        return pltpu.make_async_remote_copy(
            src_ref=src, dst_ref=dst, send_sem=ssem, recv_sem=rsem, device_id=to,
            device_id_type=MESH)

    def lane(xi, co):
        return xi * CORES + co

    def zcopy(way, b, s, own=False):
        rows = pl.ds(s * sub, sub)
        dst = pts.at[b, c, rows]
        src = train.at[c, rows] if own else dst
        to = z + 1 if way == 0 else z - 1
        return remote(src, dst, zs.at[way, b, s], zr.at[b, s], points=to)

    def xcopy(b, k, s, coming=False):
        li = lane(back[k], core) if coming else c
        ref = pts.at[b, li, pl.ds(s * sub, sub)]
        return remote(ref, ref, xs.at[b, k, s], xr.at[b, k, s], centers=lane(off[k], core))

    def ccopy(b, xi, s, coming=False):
        ref = pts.at[b, lane(xi, other if coming else core), pl.ds(s * sub, sub)]
        return remote(ref, ref, cs.at[b, xi, s], cr.at[b, xi, s], centers=mate)

    def pccopy(b, xi):
        return remote(pred.at[b, other, xi], pc.at[b, xi], pcs.at[b, xi], pcr.at[b, xi],
                      centers=mate)

    def pxcopy(b, k):
        return remote(pred.at[b, core, off[k]], px.at[b, k], pxs.at[b, k], pxr.at[b, k],
                      centers=lane(off[k], core))

    def pzcopy(b, src_z):
        return remote(psum.at[b], pz.at[src_z], pzs.at[b], pzr.at[src_z], points=b)

    def czcopy(b, to):
        ref = cot.at[b, c]
        return remote(ref, ref, czs.at[to], czr.at[b], points=to)

    def cxcopy(b, k, coming=False):
        ref = cot.at[b, lane(back[k], core) if coming else c]
        return remote(ref, ref, cxs.at[b, k], cxr.at[b, k], centers=lane(off[k], core))

    def cccopy(b, xi, coming=False):
        ref = cot.at[b, lane(xi, other if coming else core)]
        return remote(ref, ref, ccs.at[b, xi], ccr.at[b, xi], centers=mate)

    def blocks(d, f, first=1):
        @pl.when((d >= first) & (d < Z) & (z - d >= 0))
        def _():
            f(z - d)

        @pl.when((d >= max(first, 1)) & (d < Z) & (z + d < Z))
        def _():
            f(z + d)

    barrier = pltpu.get_barrier_semaphore()
    for k in range(1, Z):
        pl.semaphore_signal(barrier, inc=1, device_id={"points": lax.rem(z + k, Z)},
                            device_id_type=MESH)
    for k in range(1, X):
        pl.semaphore_signal(barrier, inc=1, device_id={"centers": lane(off[k], core)},
                            device_id_type=MESH)
    pl.semaphore_signal(barrier, inc=1, device_id={"centers": mate}, device_id_type=MESH)
    own_points = pltpu.make_async_copy(train, pts.at[z], ls.at[0])
    own_saved = pltpu.make_async_copy(saved.at[c], sv, ls.at[1])
    own_target = pltpu.make_async_copy(target.at[c], tg, ls.at[2])
    own_points.start()
    own_saved.start()
    own_target.start()
    pl.semaphore_wait(barrier, Z - 1 + X - 1 + 1)

    for s in range(SUBS):
        @pl.when(z + 1 < Z)
        def _():
            zcopy(0, z, s, own=True).start()

        @pl.when(z > 0)
        def _():
            zcopy(1, z, s, own=True).start()

    n_cen = cen.shape[0]
    cen32 = cen[...].astype(f32)
    cm2[...] = (-2.0 * cen32).astype(bf16)
    coeft[...] = coef[...].astype(f32).T.astype(bf16)
    csq[...] = jnp.broadcast_to(jnp.sum(cen32 * cen32, axis=1, keepdims=True), (n_cen, 128))
    nrate[...] = jnp.broadcast_to(rates[...] * (-LOG2E / width), (128, n_cen)).T
    gcen[...] = jnp.zeros_like(gcen)
    gcoef[...] = jnp.zeros_like(gcoef)
    tot[...] = jnp.zeros_like(tot)

    def wide(col):
        return jnp.concatenate([col] * (q // 128), axis=1)

    def forward(b):
        def piece(co, xi):
            t = lane(xi, co)
            rows_t = pts[b, t].T
            r32 = rows_t.astype(f32)
            psq = jnp.sum(r32 * r32, axis=0, keepdims=True)
            cross = jnp.dot(cm2[...], rows_t, preferred_element_type=f32)
            dist = (psq + wide(csq[...])) + cross
            k = jnp.exp2(wide(nrate[...]) * dist).astype(bf16)
            kt[b, :, pl.ds(pl.multiple_of(t * q, q), q)] = k
            pred[b, co, xi] = jnp.dot(coeft[...], k, preferred_element_type=f32)
        order = [off[k] for k in range(1, X)] + [x]
        for xi in order:
            piece(other, xi)
            pccopy(b, xi).start()
        for xi in order:
            piece(core, xi)

    def backward(b):
        for t in range(C):
            cols = slice(t * q, (t + 1) * q)
            mix = lax.dot_general(coef[...], cot[b, t], (((1,), (1,)), ((), ())),
                                  preferred_element_type=f32)
            w = (kt[b, :, cols].astype(f32) * mix).astype(bf16)
            w32 = w.astype(f32)
            part = w32[:, :128]
            for i in range(1, q // 128):
                part = part + w32[:, i * 128:(i + 1) * 128]
            tot[...] += part
            wbuf[:, cols] = w
        gcen[...] += jnp.dot(wbuf[...], pts[b].reshape(C * q, width), preferred_element_type=f32)
        gcoef[...] += jnp.dot(kt[b], cot[b].reshape(C * q, cot.shape[3]),
                              preferred_element_type=f32)

    def arrive(b, s):
        zcopy(0, b, s).wait_recv()

        @pl.when((b < z) & (z + 1 < Z))
        def _():
            zcopy(0, b, s).start()

        @pl.when((b > z) & (z > 0))
        def _():
            zcopy(1, b, s).start()
        for k in range(1, X):
            xcopy(b, k, s).start()
        ccopy(b, x, s).start()

    def cross_x(b):
        for s in range(SUBS):
            for k in range(1, X):
                xcopy(b, k, s, coming=True).wait_recv()
                ccopy(b, back[k], s).start()

    def add_core(b):
        for k in range(1, X):
            pccopy(b, off[k]).wait_recv()
            pred[b, core, off[k]] += pc[b, off[k]]
            pxcopy(b, k).start()
        pccopy(b, x).wait_recv()
        pred[b, core, x] += pc[b, x]

    def add_plane(b):
        total = pred[b, core, x]
        for k in range(1, X):
            pxcopy(b, k).wait_recv()
            total = total + px[b, k]
        psum[b] = total

        @pl.when(b != z)
        def _():
            pzcopy(b, z).start()

    def work(b):
        for xi in range(X):
            for s in range(SUBS):
                ccopy(b, xi, s, coming=True).wait_recv()
        forward(b)

    own_points.wait()
    forward(z)

    def step(d, carry):
        for s in range(SUBS):
            blocks(d, lambda b: arrive(b, s))
        pl.when(d == 1)(lambda: add_core(z))
        blocks(d - 2, add_core)
        blocks(d - 1, cross_x)
        blocks(d - 1, work)
        pl.when(d == 1)(lambda: add_plane(z))
        blocks(d - 2, add_plane)
        return carry
    lax.fori_loop(1, Z + 2, step, 0)

    total = psum[z]
    for k in range(1, Z):
        src = lax.rem(z + k, Z)
        pzcopy(src, src).wait_recv()
        total = total + pz[src]
    own_saved.wait()
    own_target.wait()
    residual = total.T + sv[...] - tg[...]
    ratio = residual / delta[...]
    cot[z, c] = (residual / jnp.sqrt(1.0 + ratio * ratio)).astype(bf16)
    for k in range(1, Z):
        czcopy(z, lax.rem(z + k, Z)).start()

    def spread_cot(b):
        for k in range(1, X):
            cxcopy(b, k).start()
        cccopy(b, x).start()

    def cot_arrive(b):
        czcopy(b, b).wait_recv()
        spread_cot(b)

    def cot_work(b):
        for k in range(1, X):
            cxcopy(b, k, coming=True).wait_recv()
            cccopy(b, back[k]).start()
        for xi in range(X):
            cccopy(b, xi, coming=True).wait_recv()
        backward(b)

    spread_cot(z)

    def cot_step(d, carry):
        blocks(d, cot_arrive)
        blocks(d - 1, cot_work, 0)
        return carry
    lax.fori_loop(1, Z + 1, cot_step, 0)

    row_totals = jnp.sum(tot[...], axis=1, keepdims=True)
    gcen[...] -= row_totals * cen[...].astype(f32)

    def drain(b, carry):
        for s in range(SUBS):
            @pl.when((b <= z) & (z + 1 < Z))
            def _():
                zcopy(0, b, s).wait_send()

            @pl.when((b >= z) & (z > 0))
            def _():
                zcopy(1, b, s).wait_send()

        @pl.when(b != z)
        def _():
            for s in range(SUBS):
                for k in range(1, X):
                    xcopy(b, k, s).wait_send()
                for xi in range(X):
                    ccopy(b, xi, s).wait_send()
            pzcopy(b, z).wait_send()
            czcopy(z, b).wait_send()
        for xi in range(X):
            pccopy(b, xi).wait_send()
        for k in range(1, X):
            pxcopy(b, k).wait_send()
            cxcopy(b, k).wait_send()
        for xi in range(X):
            cccopy(b, xi).wait_send()
        return carry
    lax.fori_loop(0, Z, drain, 0)


def per_device(Z, C, train_points, saved_preds, targets, huber_delta, center_pos, coefficients, spread):
    n_points, width = train_points.shape
    n_cen, n_out = coefficients.shape
    X, q = C // CORES, n_points // C
    vm, anywhere = pl.BlockSpec(memory_space=pltpu.VMEM), pl.BlockSpec(memory_space=pl.ANY)
    dma = pltpu.SemaphoreType.DMA
    flops = 2 * Z * n_points * n_cen * (2 * width + 3 * n_out)
    rates = spread.astype(f32)
    held = Z * n_points * (2 * width + 2 * n_cen + 12 * n_out) + (12 << 20)
    moved, grad_coef = pl.pallas_call(
        functools.partial(body, Z, C),
        out_shape=(jax.ShapeDtypeStruct((n_cen, width), f32),
                   jax.ShapeDtypeStruct((n_cen, n_out), f32)),
        in_specs=[anywhere] * 3 + [vm] * 4,
        out_specs=(vm, vm),
        scratch_shapes=[
            pltpu.VMEM((Z, C, q, width), bf16),
            pltpu.VMEM((Z, n_cen, C * q), bf16),
            pltpu.VMEM((Z, CORES, X, n_out, q), f32),
            pltpu.VMEM((Z, X, n_out, q), f32),
            pltpu.VMEM((Z, X, n_out, q), f32),
            pltpu.VMEM((Z, n_out, q), f32),
            pltpu.VMEM((Z, n_out, q), f32),
            pltpu.VMEM((Z, C, q, n_out), bf16),
            pltpu.VMEM((n_cen, width), bf16),
            pltpu.VMEM((n_out, n_cen), bf16),
            pltpu.VMEM((n_cen, 128), f32),
            pltpu.VMEM((n_cen, 128), f32),
            pltpu.VMEM((n_cen, 128), f32),
            pltpu.VMEM((n_cen, C * q), bf16),
            pltpu.VMEM((q, n_out), f32),
            pltpu.VMEM((q, n_out), f32),
            dma((2, Z, SUBS)), dma((Z, SUBS)),
            dma((Z, X, SUBS)), dma((Z, X, SUBS)),
            dma((Z, X, SUBS)), dma((Z, X, SUBS)),
            dma((Z, X)), dma((Z, X)),
            dma((Z, X)), dma((Z, X)),
            dma((Z,)), dma((Z,)),
            dma((Z,)), dma((Z,)),
            dma((Z, X)), dma((Z, X)),
            dma((Z, X)), dma((Z, X)),
            dma((3,)),
        ],
        compiler_params=pltpu.CompilerParams(
            collective_id=0, has_side_effects=True, vmem_limit_bytes=min(held, 60 << 20)),
        cost_estimate=pl.CostEstimate(
            flops=flops, bytes_accessed=4 << 20, transcendentals=Z * n_points * n_cen),
    )(train_points.reshape(C, q, width), saved_preds.reshape(C, q, n_out),
      targets.reshape(C, q, n_out), huber_delta.reshape(1, n_out),
      rates.reshape(1, n_cen), center_pos, coefficients)
    return (2.0 * rates / width)[:, None] * moved, grad_coef


def solution(mesh):
    rows = P(("groups", "points"), None)
    owned = P(("groups", "points", "centers"), None)
    return jax.shard_map(
        functools.partial(per_device, mesh.shape["points"], mesh.shape["centers"]),
        mesh=mesh,
        in_specs=(rows, rows, rows, P("groups"), owned, owned, P(("groups", "points", "centers"))),
        out_specs=(owned, owned),
        check_vma=False,
    )
```

```python
import functools

import jax
import jax.numpy as jnp
from jax import lax
from jax.experimental import pallas as pl
from jax.experimental.pallas import tpu as pltpu
from jax.sharding import PartitionSpec as P

CORES = 2
SUBS = 2
LOG2E = 1.4426950408889634
MESH = pl.DeviceIdType.MESH
f32, bf16 = jnp.float32, jnp.bfloat16


def body(Z, C, train, saved, target, delta_in, rates_in, cen_in, coef_in, gcen, gcoef,
         pts, ptst, psqs, kt, pred, pc, psum, pz, cot, cm2, coeft, csq, nrate, tot, wbuf, sv, tg,
         delta, rates, cen, coef,
         zs, zr, xs, xr, cs, cr, pcs, pcr, pzs, pzr,
         czs, czr, cxs, cxr, ccs, ccr, es, er, ls):
    X = C // CORES
    q, width = pts.shape[2], pts.shape[3]
    sub = q // SUBS
    z, c = lax.axis_index("points"), lax.axis_index("centers")
    x, core = lax.div(c, CORES), lax.rem(c, CORES)
    other = 1 - core
    mate = x * CORES + other
    off = [lax.rem(x + k, X) for k in range(X)]
    back = [lax.rem(x + X - k, X) for k in range(X)]

    def remote(src, dst, ssem, rsem, **to):
        return pltpu.make_async_remote_copy(
            src_ref=src, dst_ref=dst, send_sem=ssem, recv_sem=rsem, device_id=to,
            device_id_type=MESH)

    def lane(xi, co):
        return xi * CORES + co

    def zcopy(way, b, s, own=False):
        rows = pl.ds(s * sub, sub)
        dst = pts.at[b, c, rows]
        src = train.at[c, rows] if own else dst
        to = z + 1 if way == 0 else z - 1
        return remote(src, dst, zs.at[way, b, s], zr.at[b, s], points=to)

    def xcopy(b, k, s, coming=False):
        li = lane(back[k], core) if coming else c
        ref = pts.at[b, li, pl.ds(s * sub, sub)]
        return remote(ref, ref, xs.at[b, k, s], xr.at[b, k, s], centers=lane(off[k], core))

    def ccopy(b, xi, s, coming=False):
        ref = pts.at[b, lane(xi, other if coming else core), pl.ds(s * sub, sub)]
        return remote(ref, ref, cs.at[b, xi, s], cr.at[b, xi, s], centers=mate)

    def ecopies(k, coming=False):
        at = back[k] if coming else x
        return [remote(src, dst.at[at], es.at[k, i], er.at[k, i], centers=lane(off[k], core))
                for i, (src, dst) in enumerate(
                    ((cen_in, cen), (coef_in, coef), (rates_in, rates)))]

    def pccopy(b):
        return remote(pred.at[b, other], pc.at[b], pcs.at[b], pcr.at[b], centers=mate)

    def pzcopy(b, src_z):
        return remote(psum.at[b], pz.at[src_z], pzs.at[b], pzr.at[src_z], points=b)

    def czcopy(b, to):
        ref = cot.at[b, c]
        return remote(ref, ref, czs.at[to], czr.at[b], points=to)

    def cxcopy(b, k, coming=False):
        ref = cot.at[b, lane(back[k], core) if coming else c]
        return remote(ref, ref, cxs.at[b, k], cxr.at[b, k], centers=lane(off[k], core))

    def cccopy(b, xi, coming=False):
        ref = cot.at[b, lane(xi, other if coming else core)]
        return remote(ref, ref, ccs.at[b, xi], ccr.at[b, xi], centers=mate)

    def blocks(d, f, first=1):
        @pl.when((d >= first) & (d < Z) & (z - d >= 0))
        def _():
            f(z - d)

        @pl.when((d >= max(first, 1)) & (d < Z) & (z + d < Z))
        def _():
            f(z + d)

    barrier = pltpu.get_barrier_semaphore()
    for k in range(1, Z):
        pl.semaphore_signal(barrier, inc=1, device_id={"points": lax.rem(z + k, Z)},
                            device_id_type=MESH)
    for k in range(1, X):
        pl.semaphore_signal(barrier, inc=1, device_id={"centers": lane(off[k], core)},
                            device_id_type=MESH)
    pl.semaphore_signal(barrier, inc=1, device_id={"centers": mate}, device_id_type=MESH)
    own_points = pltpu.make_async_copy(train, pts.at[z], ls.at[0])
    own_saved = pltpu.make_async_copy(saved.at[c], sv, ls.at[1])
    own_target = pltpu.make_async_copy(target.at[c], tg, ls.at[2])
    own_points.start()
    own_saved.start()
    own_target.start()
    small = [pltpu.make_async_copy(a, b, ls.at[3 + i]) for i, (a, b) in enumerate(
        ((cen_in, cen.at[x]), (coef_in, coef.at[x]), (rates_in, rates.at[x]), (delta_in, delta)))]
    for copy in small:
        copy.start()
    pl.semaphore_wait(barrier, Z - 1 + X - 1 + 1)

    for s in range(SUBS):
        @pl.when(z + 1 < Z)
        def _():
            zcopy(0, z, s, own=True).start()

        @pl.when(z > 0)
        def _():
            zcopy(1, z, s, own=True).start()

    for k in range(1, X):
        for copy in ecopies(k):
            copy.start()

    n_cen = cen.shape[1]

    def prepare(xi):
        cen32 = cen[xi].astype(f32)
        cm2[xi] = (-2.0 * cen32).astype(bf16)
        coeft[xi] = coef[xi].astype(f32).T.astype(bf16)
        csq[xi] = jnp.broadcast_to(jnp.sum(cen32 * cen32, axis=1, keepdims=True), (n_cen, 128))
        nrate[xi] = jnp.broadcast_to(rates[xi] * (-LOG2E / width), (128, n_cen)).T

    for copy in small:
        copy.wait()
    prepare(x)
    gcen[...] = jnp.zeros_like(gcen)
    gcoef[...] = jnp.zeros_like(gcoef)
    tot[...] = jnp.zeros_like(tot)

    def wide(col):
        return jnp.concatenate([col] * (q // 128), axis=1)

    def cols_of(t):
        return pl.ds(pl.multiple_of(t * q, q), q)

    def square_sum(rows_t):
        r32 = rows_t.astype(f32)
        return jnp.sum(r32 * r32, axis=0, keepdims=True)

    def kernel_of(rows_t, psq, xi):
        cross = jnp.dot(cm2[xi], rows_t, preferred_element_type=f32)
        dist = (psq + wide(csq[xi])) + cross
        return jnp.exp2(wide(nrate[xi]) * dist).astype(bf16)

    def forward_own(b):
        for co in (other, core):
            t = lane(x, co)
            rows_t = pts[b, t].T
            psq = square_sum(rows_t)
            ptst[b, co] = rows_t
            psqs[b, co] = psq
            k = kernel_of(rows_t, psq, x)
            kt[b, :, cols_of(t)] = k
            pred[b, co] = jnp.dot(coeft[x], k, preferred_element_type=f32)

    def forward_rest(b):
        for co in (other, core):
            rows_t, psq = ptst[b, co], psqs[b, co]
            total = pred[b, co]
            for i in range(1, X):
                k = kernel_of(rows_t, psq, off[i])
                total = total + jnp.dot(coeft[off[i]], k, preferred_element_type=f32)
            pred[b, co] = total
            if co is other:
                pccopy(b).start()

    def kernel_rest(b):
        for i in range(1, X):
            for co in (core, other):
                t = lane(back[i], co)
                rows_t = pts[b, t].T
                kt[b, :, cols_of(t)] = kernel_of(rows_t, square_sum(rows_t), x)

    def backward(b):
        for t in range(C):
            cols = slice(t * q, (t + 1) * q)
            mix = lax.dot_general(coef[x], cot[b, t], (((1,), (1,)), ((), ())),
                                  preferred_element_type=f32)
            w = (kt[b, :, cols].astype(f32) * mix).astype(bf16)
            w32 = w.astype(f32)
            part = w32[:, :128]
            for i in range(1, q // 128):
                part = part + w32[:, i * 128:(i + 1) * 128]
            tot[...] += part
            wbuf[:, cols] = w
        gcen[...] += jnp.dot(wbuf[...], pts[b].reshape(C * q, width), preferred_element_type=f32)
        gcoef[...] += jnp.dot(kt[b], cot[b].reshape(C * q, cot.shape[3]),
                              preferred_element_type=f32)

    def arrive(b, s):
        zcopy(0, b, s).wait_recv()

        @pl.when((b < z) & (z + 1 < Z))
        def _():
            zcopy(0, b, s).start()

        @pl.when((b > z) & (z > 0))
        def _():
            zcopy(1, b, s).start()
        ccopy(b, x, s).start()

    def arrivals(d):
        for s in range(SUBS):
            blocks(d, lambda b: arrive(b, s))

    def send_x(b):
        for s in range(SUBS):
            for k in range(1, X):
                xcopy(b, k, s).start()

    def work(b):
        for s in range(SUBS):
            ccopy(b, x, s, coming=True).wait_recv()
        forward_own(b)

    def finish(b):
        pccopy(b).wait_recv()
        psum[b] = pred[b, core] + pc[b]

        @pl.when(b != z)
        def _():
            pzcopy(b, z).start()

    def rest(b):
        for s in range(SUBS):
            for k in range(1, X):
                xcopy(b, k, s, coming=True).wait_recv()
                ccopy(b, back[k], s).start()
        for s in range(SUBS):
            for k in range(1, X):
                ccopy(b, back[k], s, coming=True).wait_recv()
        kernel_rest(b)

    own_points.wait()
    forward_own(z)
    kernel_rest(z)

    def early(d, carry):
        arrivals(d)
        blocks(d, work)
        return carry
    lax.fori_loop(1, Z - 1, early, 0)

    for k in range(1, X):
        for copy in ecopies(k, coming=True):
            copy.wait_recv()
        prepare(back[k])

    def middle(d, carry):
        @pl.when((d >= 1) & (d < Z - 1))
        def _():
            blocks(d, send_x)

        @pl.when(d == Z - 1)
        def _():
            arrivals(d)
            blocks(d, send_x)
            blocks(d, work)
        blocks(d, forward_rest, 0)
        blocks(d - 1, finish, 0)
        return carry
    lax.fori_loop(0, Z + 1, middle, 0)

    total = psum[z]
    for k in range(1, Z):
        src = lax.rem(z + k, Z)
        pzcopy(src, src).wait_recv()
        total = total + pz[src]
    own_saved.wait()
    own_target.wait()
    residual = total.T + sv[...] - tg[...]
    ratio = residual / delta[...]
    cot[z, c] = (residual / jnp.sqrt(1.0 + ratio * ratio)).astype(bf16)
    for k in range(1, Z):
        czcopy(z, lax.rem(z + k, Z)).start()

    def spread_cot(b):
        for k in range(1, X):
            cxcopy(b, k).start()
        cccopy(b, x).start()

    def cot_arrive(b):
        czcopy(b, b).wait_recv()
        spread_cot(b)

    def cot_cross(b):
        for k in range(1, X):
            cxcopy(b, k, coming=True).wait_recv()
            cccopy(b, back[k]).start()

    def cot_work(b):
        for xi in range(X):
            cccopy(b, xi, coming=True).wait_recv()
        backward(b)

    spread_cot(z)

    def late(d, carry):
        blocks(d, rest)
        blocks(d, cot_arrive)
        return carry
    lax.fori_loop(1, Z, late, 0)

    cot_cross(z)

    def last(d, carry):
        blocks(d + 1, cot_cross)
        blocks(d, cot_work, 0)
        return carry
    lax.fori_loop(0, Z, last, 0)

    row_totals = jnp.sum(tot[...], axis=1, keepdims=True)
    scale = (-2.0 / LOG2E) * nrate[x]
    scale = jnp.concatenate([scale] * (width // 128), axis=1)
    gcen[...] = scale * (gcen[...] - row_totals * cen[x].astype(f32))

    def drain(b, carry):
        for s in range(SUBS):
            @pl.when((b <= z) & (z + 1 < Z))
            def _():
                zcopy(0, b, s).wait_send()

            @pl.when((b >= z) & (z > 0))
            def _():
                zcopy(1, b, s).wait_send()

        @pl.when(b != z)
        def _():
            for s in range(SUBS):
                for k in range(1, X):
                    xcopy(b, k, s).wait_send()
                for xi in range(X):
                    ccopy(b, xi, s).wait_send()
            pzcopy(b, z).wait_send()
            czcopy(z, b).wait_send()
        pccopy(b).wait_send()
        for k in range(1, X):
            cxcopy(b, k).wait_send()
        for xi in range(X):
            cccopy(b, xi).wait_send()
        return carry
    lax.fori_loop(0, Z, drain, 0)
    for k in range(1, X):
        for copy in ecopies(k):
            copy.wait_send()


def per_device(Z, C, train_points, saved_preds, targets, huber_delta, center_pos, coefficients, spread):
    n_points, width = train_points.shape
    n_cen, n_out = coefficients.shape
    X, q = C // CORES, n_points // C
    vm, in_hbm = pl.BlockSpec(memory_space=pltpu.VMEM), pl.BlockSpec(memory_space=pltpu.HBM)
    dma = pltpu.SemaphoreType.DMA
    flops = 2 * Z * n_points * n_cen * (2 * width + 3 * n_out)
    return tuple(pl.pallas_call(
        functools.partial(body, Z, C),
        out_shape=(jax.ShapeDtypeStruct((n_cen, width), f32),
                   jax.ShapeDtypeStruct((n_cen, n_out), f32)),
        in_specs=[in_hbm] * 7,
        out_specs=(vm, vm),
        scratch_shapes=[
            pltpu.VMEM((Z, C, q, width), bf16),
            pltpu.VMEM((Z, CORES, width, q), bf16),
            pltpu.VMEM((Z, CORES, 1, q), f32),
            pltpu.VMEM((Z, n_cen, C * q), bf16),
            pltpu.VMEM((Z, CORES, n_out, q), f32),
            pltpu.VMEM((Z, n_out, q), f32),
            pltpu.VMEM((Z, n_out, q), f32),
            pltpu.VMEM((Z, n_out, q), f32),
            pltpu.VMEM((Z, C, q, n_out), bf16),
            pltpu.VMEM((X, n_cen, width), bf16),
            pltpu.VMEM((X, n_out, n_cen), bf16),
            pltpu.VMEM((X, n_cen, 128), f32),
            pltpu.VMEM((X, n_cen, 128), f32),
            pltpu.VMEM((n_cen, 128), f32),
            pltpu.VMEM((n_cen, C * q), bf16),
            pltpu.VMEM((q, n_out), f32),
            pltpu.VMEM((q, n_out), f32),
            pltpu.VMEM((1, n_out), f32),
            pltpu.VMEM((X, 1, n_cen), f32),
            pltpu.VMEM((X, n_cen, width), bf16),
            pltpu.VMEM((X, n_cen, n_out), bf16),
            dma((2, Z, SUBS)), dma((Z, SUBS)),
            dma((Z, X, SUBS)), dma((Z, X, SUBS)),
            dma((Z, X, SUBS)), dma((Z, X, SUBS)),
            dma((Z,)), dma((Z,)),
            dma((Z,)), dma((Z,)),
            dma((Z,)), dma((Z,)),
            dma((Z, X)), dma((Z, X)),
            dma((Z, X)), dma((Z, X)),
            dma((X, 3)), dma((X, 3)),
            dma((7,)),
        ],
        compiler_params=pltpu.CompilerParams(
            collective_id=0, has_side_effects=True, vmem_limit_bytes=60 << 20),
        cost_estimate=pl.CostEstimate(
            flops=flops, bytes_accessed=4 << 20, transcendentals=Z * n_points * n_cen),
    )(train_points.reshape(C, q, width), saved_preds.reshape(C, q, n_out),
      targets.reshape(C, q, n_out), huber_delta.reshape(1, n_out),
      spread.astype(f32).reshape(1, n_cen), center_pos, coefficients))


def solution(mesh):
    rows = P(("groups", "points"), None)
    owned = P(("groups", "points", "centers"), None)
    return jax.shard_map(
        functools.partial(per_device, mesh.shape["points"], mesh.shape["centers"]),
        mesh=mesh,
        in_specs=(rows, rows, rows, P("groups"), owned, owned, P(("groups", "points", "centers"))),
        out_specs=(owned, owned),
        check_vma=False,
    )
```

```python
import functools

import jax
import jax.numpy as jnp
from jax import lax
from jax.experimental import pallas as pl
from jax.experimental.pallas import tpu as pltpu
from jax.sharding import PartitionSpec as P

CORES = 2
SUBS = 2
LOG2E = 1.4426950408889634
MESH = pl.DeviceIdType.MESH
f32, bf16 = jnp.float32, jnp.bfloat16


def body(Z, C, train, saved, target, delta_in, rates_in, cen_in, coef_in, gcen, gcoef,
         pts, ptst, psqs, kt, pred, pc, psum, pz, cot, cm2, coeft, csq, nrate, tot, wbuf, sv, tg,
         delta, rates, cen, coef,
         zs, zr, xs, xr, cs, cr, pcs, pcr, pzs, pzr,
         czs, czr, cxs, cxr, ccs, ccr, es, er, ls):
    X = C // CORES
    q, width = pts.shape[2], pts.shape[3]
    sub = q // SUBS
    z, c = lax.axis_index("points"), lax.axis_index("centers")
    x, core = lax.div(c, CORES), lax.rem(c, CORES)
    other = 1 - core
    mate = x * CORES + other
    off = [lax.rem(x + k, X) for k in range(X)]
    back = [lax.rem(x + X - k, X) for k in range(X)]

    def remote(src, dst, ssem, rsem, **to):
        return pltpu.make_async_remote_copy(
            src_ref=src, dst_ref=dst, send_sem=ssem, recv_sem=rsem, device_id=to,
            device_id_type=MESH)

    def lane(xi, co):
        return xi * CORES + co

    def zcopy(way, b, s, own=False):
        rows = pl.ds(s * sub, sub)
        dst = pts.at[b, c, rows]
        src = train.at[c, rows] if own else dst
        to = z + 1 if way == 0 else z - 1
        return remote(src, dst, zs.at[way, b, s], zr.at[b, s], points=to)

    def xcopy(b, k, s, coming=False):
        li = lane(back[k], core) if coming else c
        ref = pts.at[b, li, pl.ds(s * sub, sub)]
        return remote(ref, ref, xs.at[b, k, s], xr.at[b, k, s], centers=lane(off[k], core))

    def ccopy(b, xi, s, coming=False):
        ref = pts.at[b, lane(xi, other if coming else core), pl.ds(s * sub, sub)]
        return remote(ref, ref, cs.at[b, xi, s], cr.at[b, xi, s], centers=mate)

    def ecopies(k, coming=False):
        at = back[k] if coming else x
        return [remote(src, dst.at[at], es.at[k, i], er.at[k, i], centers=lane(off[k], core))
                for i, (src, dst) in enumerate(
                    ((cen_in, cen), (coef_in, coef), (rates_in, rates)))]

    def pccopy(b):
        return remote(pred.at[b, other], pc.at[b], pcs.at[b], pcr.at[b], centers=mate)

    def pzcopy(b, src_z):
        return remote(psum.at[b], pz.at[src_z], pzs.at[b], pzr.at[src_z], points=b)

    def czcopy(b, to):
        ref = cot.at[b, c]
        return remote(ref, ref, czs.at[to], czr.at[b], points=to)

    def cxcopy(b, k, coming=False):
        ref = cot.at[b, lane(back[k], core) if coming else c]
        return remote(ref, ref, cxs.at[b, k], cxr.at[b, k], centers=lane(off[k], core))

    def cccopy(b, xi, coming=False):
        ref = cot.at[b, lane(xi, other if coming else core)]
        return remote(ref, ref, ccs.at[b, xi], ccr.at[b, xi], centers=mate)

    def blocks(d, f, first=1):
        @pl.when((d >= first) & (d < Z) & (z - d >= 0))
        def _():
            f(z - d)

        @pl.when((d >= max(first, 1)) & (d < Z) & (z + d < Z))
        def _():
            f(z + d)

    barrier = pltpu.get_barrier_semaphore()
    for k in range(1, Z):
        pl.semaphore_signal(barrier, inc=1, device_id={"points": lax.rem(z + k, Z)},
                            device_id_type=MESH)
    for k in range(1, X):
        pl.semaphore_signal(barrier, inc=1, device_id={"centers": lane(off[k], core)},
                            device_id_type=MESH)
    pl.semaphore_signal(barrier, inc=1, device_id={"centers": mate}, device_id_type=MESH)
    own_points = pltpu.make_async_copy(train, pts.at[z], ls.at[0])
    own_saved = pltpu.make_async_copy(saved.at[c], sv, ls.at[1])
    own_target = pltpu.make_async_copy(target.at[c], tg, ls.at[2])
    own_points.start()
    own_saved.start()
    own_target.start()
    small = [pltpu.make_async_copy(a, b, ls.at[3 + i]) for i, (a, b) in enumerate(
        ((cen_in, cen.at[x]), (coef_in, coef.at[x]), (rates_in, rates.at[x]), (delta_in, delta)))]
    for copy in small:
        copy.start()
    pl.semaphore_wait(barrier, Z - 1 + X - 1 + 1)

    for s in range(SUBS):
        @pl.when(z + 1 < Z)
        def _():
            zcopy(0, z, s, own=True).start()

        @pl.when(z > 0)
        def _():
            zcopy(1, z, s, own=True).start()

    for k in range(1, X):
        for copy in ecopies(k):
            copy.start()

    n_cen = cen.shape[1]

    def prepare(xi):
        cen32 = cen[xi].astype(f32)
        cm2[xi] = (-2.0 * cen32).astype(bf16)
        coeft[xi] = coef[xi].astype(f32).T.astype(bf16)
        csq[xi] = jnp.broadcast_to(jnp.sum(cen32 * cen32, axis=1, keepdims=True), (n_cen, 128))
        nrate[xi] = jnp.broadcast_to(rates[xi] * (-LOG2E / width), (128, n_cen)).T

    for copy in small:
        copy.wait()
    prepare(x)
    gcen[...] = jnp.zeros_like(gcen)
    gcoef[...] = jnp.zeros_like(gcoef)
    tot[...] = jnp.zeros_like(tot)

    def wide(col):
        return jnp.concatenate([col] * (q // 128), axis=1)

    def cols_of(t):
        return pl.ds(pl.multiple_of(t * q, q), q)

    def square_sum(rows_t):
        r32 = rows_t.astype(f32)
        return jnp.sum(r32 * r32, axis=0, keepdims=True)

    def kernel_of(rows_t, psq, xi):
        cross = jnp.dot(cm2[xi], rows_t, preferred_element_type=f32)
        dist = (psq + wide(csq[xi])) + cross
        return jnp.exp2(wide(nrate[xi]) * dist).astype(bf16)

    def forward_own(b):
        for co in (other, core):
            t = lane(x, co)
            rows_t = pts[b, t].T
            psq = square_sum(rows_t)
            ptst[b, co] = rows_t
            psqs[b, co] = psq
            k = kernel_of(rows_t, psq, x)
            kt[b, :, cols_of(t)] = k
            pred[b, co] = jnp.dot(coeft[x], k, preferred_element_type=f32)

    def forward_rest(b):
        for co in (other, core):
            rows_t, psq = ptst[b, co], psqs[b, co]
            total = pred[b, co]
            for i in range(1, X):
                k = kernel_of(rows_t, psq, off[i])
                total = total + jnp.dot(coeft[off[i]], k, preferred_element_type=f32)
            pred[b, co] = total
            if co is other:
                pccopy(b).start()

    def kernel_rest(b):
        for i in range(1, X):
            for co in (core, other):
                t = lane(back[i], co)
                rows_t = pts[b, t].T
                kt[b, :, cols_of(t)] = kernel_of(rows_t, square_sum(rows_t), x)

    def backward(b):
        for t in range(C):
            cols = slice(t * q, (t + 1) * q)
            mix = lax.dot_general(coef[x], cot[b, t], (((1,), (1,)), ((), ())),
                                  preferred_element_type=f32)
            w = (kt[b, :, cols].astype(f32) * mix).astype(bf16)
            w32 = w.astype(f32)
            part = w32[:, :128]
            for i in range(1, q // 128):
                part = part + w32[:, i * 128:(i + 1) * 128]
            tot[...] += part
            wbuf[:, cols] = w
        gcen[...] += jnp.dot(wbuf[...], pts[b].reshape(C * q, width), preferred_element_type=f32)
        gcoef[...] += jnp.dot(kt[b], cot[b].reshape(C * q, cot.shape[3]),
                              preferred_element_type=f32)

    def arrive(b, s):
        zcopy(0, b, s).wait_recv()

        @pl.when((b < z) & (z + 1 < Z))
        def _():
            zcopy(0, b, s).start()

        @pl.when((b > z) & (z > 0))
        def _():
            zcopy(1, b, s).start()
        ccopy(b, x, s).start()

    def arrivals(d):
        for s in range(SUBS):
            blocks(d, lambda b: arrive(b, s))

    def send_x(b):
        for s in range(SUBS):
            for k in range(1, X):
                xcopy(b, k, s).start()

    def own_lanes(b):
        for s in range(SUBS):
            ccopy(b, x, s, coming=True).wait_recv()

    def work(b):
        own_lanes(b)
        forward_own(b)

    def forward_all(b):
        own_lanes(b)
        for co in (other, core):
            t = lane(x, co)
            rows_t = pts[b, t].T
            psq = square_sum(rows_t)
            k = kernel_of(rows_t, psq, x)
            kt[b, :, cols_of(t)] = k
            total = jnp.dot(coeft[x], k, preferred_element_type=f32)
            for i in range(1, X):
                k = kernel_of(rows_t, psq, off[i])
                total = total + jnp.dot(coeft[off[i]], k, preferred_element_type=f32)
            pred[b, co] = total
            if co is other:
                pccopy(b).start()

    def finish(b):
        pccopy(b).wait_recv()
        psum[b] = pred[b, core] + pc[b]

        @pl.when(b != z)
        def _():
            pzcopy(b, z).start()

    def rest(b):
        for s in range(SUBS):
            for k in range(1, X):
                xcopy(b, k, s, coming=True).wait_recv()
                ccopy(b, back[k], s).start()
        for s in range(SUBS):
            for k in range(1, X):
                ccopy(b, back[k], s, coming=True).wait_recv()
        kernel_rest(b)

    own_points.wait()
    forward_own(z)
    kernel_rest(z)

    def early(d, carry):
        arrivals(d)
        blocks(d, work)
        return carry
    lax.fori_loop(1, Z - 1, early, 0)

    for k in range(1, X):
        for copy in ecopies(k, coming=True):
            copy.wait_recv()
        prepare(back[k])

    def middle(d, carry):
        blocks(d, send_x)
        blocks(d, forward_rest, 0)
        blocks(d - 1, finish, 0)
        return carry
    lax.fori_loop(0, Z - 1, middle, 0)
    blocks(Z - 2, finish, 0)
    arrivals(Z - 1)
    blocks(Z - 1, send_x)
    blocks(Z - 1, forward_all)
    blocks(Z - 1, finish)
    blocks(1, rest)

    total = psum[z]
    for k in range(1, Z):
        src = lax.rem(z + k, Z)
        pzcopy(src, src).wait_recv()
        total = total + pz[src]
    own_saved.wait()
    own_target.wait()
    residual = total.T + sv[...] - tg[...]
    ratio = residual / delta[...]
    cot[z, c] = (residual / jnp.sqrt(1.0 + ratio * ratio)).astype(bf16)
    for k in range(1, Z):
        czcopy(z, lax.rem(z + k, Z)).start()

    def spread_cot(b):
        for k in range(1, X):
            cxcopy(b, k).start()
        cccopy(b, x).start()

    def cot_arrive(b):
        czcopy(b, b).wait_recv()
        spread_cot(b)

    def cot_cross(b):
        for k in range(1, X):
            cxcopy(b, k, coming=True).wait_recv()
            cccopy(b, back[k]).start()

    def cot_work(b):
        for xi in range(X):
            cccopy(b, xi, coming=True).wait_recv()
        backward(b)

    spread_cot(z)

    blocks(2, rest)
    blocks(1, cot_arrive)
    cot_cross(z)
    cot_work(z)

    def late(d, carry):
        blocks(d - 1, cot_arrive)
        blocks(d, rest)
        return carry
    lax.fori_loop(3, Z + 1, late, 0)
    blocks(1, cot_cross)

    def last(d, carry):
        blocks(d + 1, cot_cross)
        blocks(d, cot_work)
        return carry
    lax.fori_loop(1, Z, last, 0)

    row_totals = jnp.sum(tot[...], axis=1, keepdims=True)
    scale = (-2.0 / LOG2E) * nrate[x]
    scale = jnp.concatenate([scale] * (width // 128), axis=1)
    gcen[...] = scale * (gcen[...] - row_totals * cen[x].astype(f32))

    def drain(b, carry):
        for s in range(SUBS):
            @pl.when((b <= z) & (z + 1 < Z))
            def _():
                zcopy(0, b, s).wait_send()

            @pl.when((b >= z) & (z > 0))
            def _():
                zcopy(1, b, s).wait_send()

        @pl.when(b != z)
        def _():
            for s in range(SUBS):
                for k in range(1, X):
                    xcopy(b, k, s).wait_send()
                for xi in range(X):
                    ccopy(b, xi, s).wait_send()
            pzcopy(b, z).wait_send()
            czcopy(z, b).wait_send()
        pccopy(b).wait_send()
        for k in range(1, X):
            cxcopy(b, k).wait_send()
        for xi in range(X):
            cccopy(b, xi).wait_send()
        return carry
    lax.fori_loop(0, Z, drain, 0)
    for k in range(1, X):
        for copy in ecopies(k):
            copy.wait_send()


def per_device(Z, C, train_points, saved_preds, targets, huber_delta, center_pos, coefficients, spread):
    n_points, width = train_points.shape
    n_cen, n_out = coefficients.shape
    X, q = C // CORES, n_points // C
    vm, in_hbm = pl.BlockSpec(memory_space=pltpu.VMEM), pl.BlockSpec(memory_space=pltpu.HBM)
    dma = pltpu.SemaphoreType.DMA
    flops = 2 * Z * n_points * n_cen * (2 * width + 3 * n_out)
    return tuple(pl.pallas_call(
        functools.partial(body, Z, C),
        out_shape=(pltpu.VMEM((n_cen, width), f32), pltpu.VMEM((n_cen, n_out), f32)),
        in_specs=[in_hbm] * 7,
        out_specs=(vm, vm),
        scratch_shapes=[
            pltpu.VMEM((Z, C, q, width), bf16),
            pltpu.VMEM((Z, CORES, width, q), bf16),
            pltpu.VMEM((Z, CORES, 1, q), f32),
            pltpu.VMEM((Z, n_cen, C * q), bf16),
            pltpu.VMEM((Z, CORES, n_out, q), f32),
            pltpu.VMEM((Z, n_out, q), f32),
            pltpu.VMEM((Z, n_out, q), f32),
            pltpu.VMEM((Z, n_out, q), f32),
            pltpu.VMEM((Z, C, q, n_out), bf16),
            pltpu.VMEM((X, n_cen, width), bf16),
            pltpu.VMEM((X, n_out, n_cen), bf16),
            pltpu.VMEM((X, n_cen, 128), f32),
            pltpu.VMEM((X, n_cen, 128), f32),
            pltpu.VMEM((n_cen, 128), f32),
            pltpu.VMEM((n_cen, C * q), bf16),
            pltpu.VMEM((q, n_out), f32),
            pltpu.VMEM((q, n_out), f32),
            pltpu.VMEM((1, n_out), f32),
            pltpu.VMEM((X, 1, n_cen), f32),
            pltpu.VMEM((X, n_cen, width), bf16),
            pltpu.VMEM((X, n_cen, n_out), bf16),
            dma((2, Z, SUBS)), dma((Z, SUBS)),
            dma((Z, X, SUBS)), dma((Z, X, SUBS)),
            dma((Z, X, SUBS)), dma((Z, X, SUBS)),
            dma((Z,)), dma((Z,)),
            dma((Z,)), dma((Z,)),
            dma((Z,)), dma((Z,)),
            dma((Z, X)), dma((Z, X)),
            dma((Z, X)), dma((Z, X)),
            dma((X, 3)), dma((X, 3)),
            dma((7,)),
        ],
        compiler_params=pltpu.CompilerParams(
            collective_id=0, has_side_effects=True, vmem_limit_bytes=60 << 20),
        cost_estimate=pl.CostEstimate(
            flops=flops, bytes_accessed=4 << 20, transcendentals=Z * n_points * n_cen),
    )(train_points.reshape(C, q, width), saved_preds.reshape(C, q, n_out),
      targets.reshape(C, q, n_out), huber_delta.reshape(1, n_out),
      spread.astype(f32).reshape(1, n_cen), center_pos, coefficients))


def solution(mesh):
    rows = P(("groups", "points"), None)
    owned = P(("groups", "points", "centers"), None)
    return jax.shard_map(
        functools.partial(per_device, mesh.shape["points"], mesh.shape["centers"]),
        mesh=mesh,
        in_specs=(rows, rows, rows, P("groups"), owned, owned, P(("groups", "points", "centers"))),
        out_specs=(owned, owned),
        check_vma=False,
    )
```

```python
import functools

import jax
import jax.numpy as jnp
from jax import lax
from jax.experimental import pallas as pl
from jax.experimental.pallas import tpu as pltpu
from jax.sharding import PartitionSpec as P

CORES = 2
SUBS = 2
LOG2E = 1.4426950408889634
MESH = pl.DeviceIdType.MESH
f32, bf16 = jnp.float32, jnp.bfloat16


def body(Z, C, train, saved, target, delta_in, rates_in, cen_in, coef_in, gcen, gcoef,
         pts, ptst, psqs, kt, pred, pc, psum, pz, cot, cm2, coeft, csq, nrate, tot, wbuf, sv, tg,
         delta, rates, cen, coef,
         zs, zr, xs, xr, cs, cr, pcs, pcr, pzs, pzr,
         czs, czr, cxs, cxr, ccs, ccr, es, er, ls):
    X = C // CORES
    q, width = pts.shape[2], pts.shape[3]
    sub = q // SUBS
    z, c = lax.axis_index("points"), lax.axis_index("centers")
    x, core = lax.div(c, CORES), lax.rem(c, CORES)
    other = 1 - core
    mate = x * CORES + other
    off = [lax.rem(x + k, X) for k in range(X)]
    back = [lax.rem(x + X - k, X) for k in range(X)]

    def remote(src, dst, ssem, rsem, **to):
        return pltpu.make_async_remote_copy(
            src_ref=src, dst_ref=dst, send_sem=ssem, recv_sem=rsem, device_id=to,
            device_id_type=MESH)

    def lane(xi, co):
        return xi * CORES + co

    def zcopy(way, b, s, own=False):
        rows = pl.ds(s * sub, sub)
        dst = pts.at[b, c, rows]
        src = train.at[c, rows] if own else dst
        to = z + 1 if way == 0 else z - 1
        return remote(src, dst, zs.at[way, b, s], zr.at[b, s], points=to)

    def xcopy(b, k, s, coming=False):
        li = lane(back[k], core) if coming else c
        ref = pts.at[b, li, pl.ds(s * sub, sub)]
        return remote(ref, ref, xs.at[b, k, s], xr.at[b, k, s], centers=lane(off[k], core))

    def ccopy(b, xi, s, coming=False):
        ref = pts.at[b, lane(xi, other if coming else core), pl.ds(s * sub, sub)]
        return remote(ref, ref, cs.at[b, xi, s], cr.at[b, xi, s], centers=mate)

    def ecopies(k, coming=False):
        at = back[k] if coming else x
        return [remote(src, dst.at[at], es.at[k, i], er.at[k, i], centers=lane(off[k], core))
                for i, (src, dst) in enumerate(
                    ((cen_in, cen), (coef_in, coef), (rates_in, rates)))]

    def pccopy(b):
        return remote(pred.at[b, other], pc.at[b], pcs.at[b], pcr.at[b], centers=mate)

    def pzcopy(b, src_z):
        return remote(psum.at[b], pz.at[src_z], pzs.at[b], pzr.at[src_z], points=b)

    def czcopy(b, to):
        ref = cot.at[b, c]
        return remote(ref, ref, czs.at[to], czr.at[b], points=to)

    def cxcopy(b, k, coming=False):
        ref = cot.at[b, lane(back[k], core) if coming else c]
        return remote(ref, ref, cxs.at[b, k], cxr.at[b, k], centers=lane(off[k], core))

    def cccopy(b, xi, coming=False):
        ref = cot.at[b, lane(xi, other if coming else core)]
        return remote(ref, ref, ccs.at[b, xi], ccr.at[b, xi], centers=mate)

    def blocks(d, f, first=1):
        @pl.when((d >= first) & (d < Z) & (z - d >= 0))
        def _():
            f(z - d)

        @pl.when((d >= max(first, 1)) & (d < Z) & (z + d < Z))
        def _():
            f(z + d)

    barrier = pltpu.get_barrier_semaphore()
    for k in range(1, Z):
        pl.semaphore_signal(barrier, inc=1, device_id={"points": lax.rem(z + k, Z)},
                            device_id_type=MESH)
    for k in range(1, X):
        pl.semaphore_signal(barrier, inc=1, device_id={"centers": lane(off[k], core)},
                            device_id_type=MESH)
    pl.semaphore_signal(barrier, inc=1, device_id={"centers": mate}, device_id_type=MESH)
    own_points = pltpu.make_async_copy(train, pts.at[z], ls.at[0])
    own_saved = pltpu.make_async_copy(saved.at[c], sv, ls.at[1])
    own_target = pltpu.make_async_copy(target.at[c], tg, ls.at[2])
    own_points.start()
    own_saved.start()
    own_target.start()
    small = [pltpu.make_async_copy(a, b, ls.at[3 + i]) for i, (a, b) in enumerate(
        ((cen_in, cen.at[x]), (coef_in, coef.at[x]), (rates_in, rates.at[x]), (delta_in, delta)))]
    for copy in small:
        copy.start()
    pl.semaphore_wait(barrier, Z - 1 + X - 1 + 1)

    for s in range(SUBS):
        @pl.when(z + 1 < Z)
        def _():
            zcopy(0, z, s, own=True).start()

        @pl.when(z > 0)
        def _():
            zcopy(1, z, s, own=True).start()

    for k in range(1, X):
        for copy in ecopies(k):
            copy.start()

    n_cen = cen.shape[1]

    def prepare(xi):
        cen32 = cen[xi].astype(f32)
        cm2[xi] = (-2.0 * cen32).astype(bf16)
        coeft[xi] = coef[xi].astype(f32).T.astype(bf16)
        csq[xi] = jnp.broadcast_to(jnp.sum(cen32 * cen32, axis=1, keepdims=True), (n_cen, 128))
        nrate[xi] = jnp.broadcast_to(rates[xi] * (-LOG2E / width), (128, n_cen)).T

    for copy in small:
        copy.wait()
    prepare(x)
    gcen[...] = jnp.zeros_like(gcen)
    gcoef[...] = jnp.zeros_like(gcoef)
    tot[...] = jnp.zeros_like(tot)

    def wide(col):
        return jnp.concatenate([col] * (q // 128), axis=1)

    def cols_of(t):
        return pl.ds(pl.multiple_of(t * q, q), q)

    def square_sum(rows_t):
        r32 = rows_t.astype(f32)
        return jnp.sum(r32 * r32, axis=0, keepdims=True)

    def kernel_of(rows_t, psq, xi):
        cross = jnp.dot(cm2[xi], rows_t, preferred_element_type=f32)
        dist = (psq + wide(csq[xi])) + cross
        return jnp.exp2(wide(nrate[xi]) * dist).astype(bf16)

    def forward_own(b):
        for co in (other, core):
            t = lane(x, co)
            rows_t = pts[b, t].T
            psq = square_sum(rows_t)
            ptst[b, co] = rows_t
            psqs[b, co] = psq
            k = kernel_of(rows_t, psq, x)
            kt[b, :, cols_of(t)] = k
            pred[b, co] = jnp.dot(coeft[x], k, preferred_element_type=f32)

    def forward_rest(b):
        for co in (other, core):
            rows_t, psq = ptst[b, co], psqs[b, co]
            total = pred[b, co]
            for i in range(1, X):
                k = kernel_of(rows_t, psq, off[i])
                total = total + jnp.dot(coeft[off[i]], k, preferred_element_type=f32)
            pred[b, co] = total
            if co is other:
                pccopy(b).start()

    def kernel_rest(b):
        for i in range(1, X):
            for co in (core, other):
                t = lane(back[i], co)
                rows_t = pts[b, t].T
                kt[b, :, cols_of(t)] = kernel_of(rows_t, square_sum(rows_t), x)

    def backward(b):
        for t in range(C):
            cols = slice(t * q, (t + 1) * q)
            mix = lax.dot_general(coef[x], cot[b, t], (((1,), (1,)), ((), ())),
                                  preferred_element_type=f32)
            w = (kt[b, :, cols].astype(f32) * mix).astype(bf16)
            w32 = w.astype(f32)
            part = w32[:, :128]
            for i in range(1, q // 128):
                part = part + w32[:, i * 128:(i + 1) * 128]
            tot[...] += part
            wbuf[:, cols] = w
        gcen[...] += jnp.dot(wbuf[...], pts[b].reshape(C * q, width), preferred_element_type=f32)
        gcoef[...] += jnp.dot(kt[b], cot[b].reshape(C * q, cot.shape[3]),
                              preferred_element_type=f32)

    def arrive(b, s):
        zcopy(0, b, s).wait_recv()

        @pl.when((b < z) & (z + 1 < Z))
        def _():
            zcopy(0, b, s).start()

        @pl.when((b > z) & (z > 0))
        def _():
            zcopy(1, b, s).start()
        ccopy(b, x, s).start()

    def arrivals(d):
        for s in range(SUBS):
            blocks(d, lambda b: arrive(b, s))

    def send_x(b):
        for s in range(SUBS):
            for k in range(1, X):
                xcopy(b, k, s).start()

    def own_lanes(b):
        for s in range(SUBS):
            ccopy(b, x, s, coming=True).wait_recv()

    def work(b):
        own_lanes(b)
        forward_own(b)

    def forward_all(b):
        own_lanes(b)
        for co in (other, core):
            t = lane(x, co)
            rows_t = pts[b, t].T
            psq = square_sum(rows_t)
            k = kernel_of(rows_t, psq, x)
            kt[b, :, cols_of(t)] = k
            total = jnp.dot(coeft[x], k, preferred_element_type=f32)
            for i in range(1, X):
                k = kernel_of(rows_t, psq, off[i])
                total = total + jnp.dot(coeft[off[i]], k, preferred_element_type=f32)
            pred[b, co] = total
            if co is other:
                pccopy(b).start()

    def finish(b):
        pccopy(b).wait_recv()
        psum[b] = pred[b, core] + pc[b]

        @pl.when(b != z)
        def _():
            pzcopy(b, z).start()

    def rest(b):
        for s in range(SUBS):
            for k in range(1, X):
                xcopy(b, k, s, coming=True).wait_recv()
                ccopy(b, back[k], s).start()
        for s in range(SUBS):
            for k in range(1, X):
                ccopy(b, back[k], s, coming=True).wait_recv()
        kernel_rest(b)

    own_points.wait()
    forward_own(z)
    kernel_rest(z)

    def early(d, carry):
        arrivals(d)
        blocks(d, work)
        return carry
    lax.fori_loop(1, Z - 1, early, 0)

    for k in range(1, X):
        for copy in ecopies(k, coming=True):
            copy.wait_recv()

    def send_early(d, carry):
        blocks(d, send_x)
        return carry
    lax.fori_loop(1, Z - 1, send_early, 0)
    for k in range(1, X):
        prepare(back[k])

    def middle(d, carry):
        blocks(d, forward_rest, 0)
        blocks(d - 1, finish, 0)
        return carry
    lax.fori_loop(0, Z - 1, middle, 0)
    blocks(Z - 2, finish, 0)
    arrivals(Z - 1)
    blocks(Z - 1, send_x)
    blocks(Z - 1, forward_all)
    blocks(Z - 1, finish)

    total = psum[z]
    for k in range(1, Z):
        src = lax.rem(z + k, Z)
        pzcopy(src, src).wait_recv()
        total = total + pz[src]
    own_saved.wait()
    own_target.wait()
    residual = total.T + sv[...] - tg[...]
    ratio = residual / delta[...]
    cot[z, c] = (residual / jnp.sqrt(1.0 + ratio * ratio)).astype(bf16)
    for k in range(1, Z):
        czcopy(z, lax.rem(z + k, Z)).start()

    def spread_cot(b):
        for k in range(1, X):
            cxcopy(b, k).start()
        cccopy(b, x).start()

    def cot_arrive(b):
        czcopy(b, b).wait_recv()
        spread_cot(b)

    def cot_cross(b):
        for k in range(1, X):
            cxcopy(b, k, coming=True).wait_recv()
            cccopy(b, back[k]).start()

    def cot_work(b):
        for xi in range(X):
            cccopy(b, xi, coming=True).wait_recv()
        backward(b)

    spread_cot(z)

    blocks(1, rest)
    blocks(1, cot_arrive)
    blocks(2, cot_arrive)
    cot_cross(z)
    cot_work(z)

    def late(d, carry):
        blocks(d, cot_arrive)
        return carry
    lax.fori_loop(3, Z, late, 0)

    def last(d, carry):
        blocks(d, cot_cross)
        blocks(d + 1, rest)
        blocks(d, cot_work)
        return carry
    lax.fori_loop(1, Z, last, 0)

    row_totals = jnp.sum(tot[...], axis=1, keepdims=True)
    scale = (-2.0 / LOG2E) * nrate[x]
    scale = jnp.concatenate([scale] * (width // 128), axis=1)
    gcen[...] = scale * (gcen[...] - row_totals * cen[x].astype(f32))

    def drain(b, carry):
        for s in range(SUBS):
            @pl.when((b <= z) & (z + 1 < Z))
            def _():
                zcopy(0, b, s).wait_send()

            @pl.when((b >= z) & (z > 0))
            def _():
                zcopy(1, b, s).wait_send()

        @pl.when(b != z)
        def _():
            for s in range(SUBS):
                for k in range(1, X):
                    xcopy(b, k, s).wait_send()
                for xi in range(X):
                    ccopy(b, xi, s).wait_send()
            pzcopy(b, z).wait_send()
            czcopy(z, b).wait_send()
        pccopy(b).wait_send()
        for k in range(1, X):
            cxcopy(b, k).wait_send()
        for xi in range(X):
            cccopy(b, xi).wait_send()
        return carry
    lax.fori_loop(0, Z, drain, 0)
    for k in range(1, X):
        for copy in ecopies(k):
            copy.wait_send()


def per_device(Z, C, train_points, saved_preds, targets, huber_delta, center_pos, coefficients, spread):
    n_points, width = train_points.shape
    n_cen, n_out = coefficients.shape
    X, q = C // CORES, n_points // C
    vm, in_hbm = pl.BlockSpec(memory_space=pltpu.VMEM), pl.BlockSpec(memory_space=pltpu.HBM)
    dma = pltpu.SemaphoreType.DMA
    flops = 2 * Z * n_points * n_cen * (2 * width + 3 * n_out)
    return tuple(pl.pallas_call(
        functools.partial(body, Z, C),
        out_shape=(pltpu.VMEM((n_cen, width), f32), pltpu.VMEM((n_cen, n_out), f32)),
        in_specs=[in_hbm] * 7,
        out_specs=(vm, vm),
        scratch_shapes=[
            pltpu.VMEM((Z, C, q, width), bf16),
            pltpu.VMEM((Z, CORES, width, q), bf16),
            pltpu.VMEM((Z, CORES, 1, q), f32),
            pltpu.VMEM((Z, n_cen, C * q), bf16),
            pltpu.VMEM((Z, CORES, n_out, q), f32),
            pltpu.VMEM((Z, n_out, q), f32),
            pltpu.VMEM((Z, n_out, q), f32),
            pltpu.VMEM((Z, n_out, q), f32),
            pltpu.VMEM((Z, C, q, n_out), bf16),
            pltpu.VMEM((X, n_cen, width), bf16),
            pltpu.VMEM((X, n_out, n_cen), bf16),
            pltpu.VMEM((X, n_cen, 128), f32),
            pltpu.VMEM((X, n_cen, 128), f32),
            pltpu.VMEM((n_cen, 128), f32),
            pltpu.VMEM((n_cen, C * q), bf16),
            pltpu.VMEM((q, n_out), f32),
            pltpu.VMEM((q, n_out), f32),
            pltpu.VMEM((1, n_out), f32),
            pltpu.VMEM((X, 1, n_cen), f32),
            pltpu.VMEM((X, n_cen, width), bf16),
            pltpu.VMEM((X, n_cen, n_out), bf16),
            dma((2, Z, SUBS)), dma((Z, SUBS)),
            dma((Z, X, SUBS)), dma((Z, X, SUBS)),
            dma((Z, X, SUBS)), dma((Z, X, SUBS)),
            dma((Z,)), dma((Z,)),
            dma((Z,)), dma((Z,)),
            dma((Z,)), dma((Z,)),
            dma((Z, X)), dma((Z, X)),
            dma((Z, X)), dma((Z, X)),
            dma((X, 3)), dma((X, 3)),
            dma((7,)),
        ],
        compiler_params=pltpu.CompilerParams(
            collective_id=0, has_side_effects=True, vmem_limit_bytes=60 << 20),
        cost_estimate=pl.CostEstimate(
            flops=flops, bytes_accessed=4 << 20, transcendentals=Z * n_points * n_cen),
    )(train_points.reshape(C, q, width), saved_preds.reshape(C, q, n_out),
      targets.reshape(C, q, n_out), huber_delta.reshape(1, n_out),
      spread.astype(f32).reshape(1, n_cen), center_pos, coefficients))


def solution(mesh):
    rows = P(("groups", "points"), None)
    owned = P(("groups", "points", "centers"), None)
    return jax.shard_map(
        functools.partial(per_device, mesh.shape["points"], mesh.shape["centers"]),
        mesh=mesh,
        in_specs=(rows, rows, rows, P("groups"), owned, owned, P(("groups", "points", "centers"))),
        out_specs=(owned, owned),
        check_vma=False,
    )
```

```python
import functools

import jax
import jax.numpy as jnp
from jax import lax
from jax.experimental import pallas as pl
from jax.experimental.pallas import tpu as pltpu
from jax.sharding import PartitionSpec as P

CORES = 2
SUBS = 2
LOG2E = 1.4426950408889634
MESH = pl.DeviceIdType.MESH
f32, bf16 = jnp.float32, jnp.bfloat16


def body(Z, C, train, saved, target, delta_in, rates_in, cen_in, coef_in, gcen, gcoef,
         pts, ptst, psqs, kt, pred, pc, psum, pz, cot, cm2, coeft, csq, nrate, tot, wbuf, sv, tg,
         delta, rates, cen, coef,
         zs, zr, xs, xr, cs, cr, pcs, pcr, pzs, pzr,
         czs, czr, cxs, cxr, ccs, ccr, es, er, ls):
    X = C // CORES
    q, width = pts.shape[2], pts.shape[3]
    sub = q // SUBS
    z, c = lax.axis_index("points"), lax.axis_index("centers")
    x, core = lax.div(c, CORES), lax.rem(c, CORES)
    other = 1 - core
    mate = x * CORES + other
    off = [lax.rem(x + k, X) for k in range(X)]
    back = [lax.rem(x + X - k, X) for k in range(X)]

    def remote(src, dst, ssem, rsem, **to):
        return pltpu.make_async_remote_copy(
            src_ref=src, dst_ref=dst, send_sem=ssem, recv_sem=rsem, device_id=to,
            device_id_type=MESH)

    def lane(xi, co):
        return xi * CORES + co

    def zcopy(way, b, s, own=False):
        rows = pl.ds(s * sub, sub)
        dst = pts.at[b, c, rows]
        src = train.at[c, rows] if own else dst
        to = z + 1 if way == 0 else z - 1
        return remote(src, dst, zs.at[way, b, s], zr.at[b, s], points=to)

    def xcopy(b, k, s, coming=False):
        li = lane(back[k], core) if coming else c
        ref = pts.at[b, li, pl.ds(s * sub, sub)]
        return remote(ref, ref, xs.at[b, k, s], xr.at[b, k, s], centers=lane(off[k], core))

    def ccopy(b, xi, s, coming=False):
        ref = pts.at[b, lane(xi, other if coming else core), pl.ds(s * sub, sub)]
        return remote(ref, ref, cs.at[b, xi, s], cr.at[b, xi, s], centers=mate)

    def ecopies(k, coming=False):
        at = back[k] if coming else x
        return [remote(src, dst.at[at], es.at[k, i], er.at[k, i], centers=lane(off[k], core))
                for i, (src, dst) in enumerate(
                    ((cen_in, cen), (coef_in, coef), (rates_in, rates)))]

    def pccopy(b):
        return remote(pred.at[b, other], pc.at[b], pcs.at[b], pcr.at[b], centers=mate)

    def pzcopy(b, src_z):
        return remote(psum.at[b], pz.at[src_z], pzs.at[b], pzr.at[src_z], points=b)

    def czcopy(b, to):
        ref = cot.at[b, c]
        return remote(ref, ref, czs.at[to], czr.at[b], points=to)

    def cxcopy(b, k, coming=False):
        ref = cot.at[b, lane(back[k], core) if coming else c]
        return remote(ref, ref, cxs.at[b, k], cxr.at[b, k], centers=lane(off[k], core))

    def cccopy(b, xi, coming=False):
        ref = cot.at[b, lane(xi, other if coming else core)]
        return remote(ref, ref, ccs.at[b, xi], ccr.at[b, xi], centers=mate)

    def blocks(d, f, first=1):
        @pl.when((d >= first) & (d < Z) & (z - d >= 0))
        def _():
            f(z - d)

        @pl.when((d >= max(first, 1)) & (d < Z) & (z + d < Z))
        def _():
            f(z + d)

    barrier = pltpu.get_barrier_semaphore()
    for k in range(1, Z):
        pl.semaphore_signal(barrier, inc=1, device_id={"points": lax.rem(z + k, Z)},
                            device_id_type=MESH)
    for k in range(1, X):
        pl.semaphore_signal(barrier, inc=1, device_id={"centers": lane(off[k], core)},
                            device_id_type=MESH)
    pl.semaphore_signal(barrier, inc=1, device_id={"centers": mate}, device_id_type=MESH)
    own_points = pltpu.make_async_copy(train, pts.at[z], ls.at[0])
    own_saved = pltpu.make_async_copy(saved.at[c], sv, ls.at[1])
    own_target = pltpu.make_async_copy(target.at[c], tg, ls.at[2])
    own_points.start()
    own_saved.start()
    own_target.start()
    small = [pltpu.make_async_copy(a, b, ls.at[3 + i]) for i, (a, b) in enumerate(
        ((cen_in, cen.at[x]), (coef_in, coef.at[x]), (rates_in, rates.at[x]), (delta_in, delta)))]
    for copy in small:
        copy.start()
    pl.semaphore_wait(barrier, Z - 1 + X - 1 + 1)

    for s in range(SUBS):
        @pl.when(z + 1 < Z)
        def _():
            zcopy(0, z, s, own=True).start()

        @pl.when(z > 0)
        def _():
            zcopy(1, z, s, own=True).start()

    for k in range(1, X):
        for copy in ecopies(k):
            copy.start()

    n_cen = cen.shape[1]

    def prepare(xi):
        cen32 = cen[xi].astype(f32)
        cm2[xi] = (-2.0 * cen32).astype(bf16)
        coeft[xi] = coef[xi].astype(f32).T.astype(bf16)
        csq[xi] = jnp.broadcast_to(jnp.sum(cen32 * cen32, axis=1, keepdims=True), (n_cen, 128))
        nrate[xi] = jnp.broadcast_to(rates[xi] * (-LOG2E / width), (128, n_cen)).T

    for copy in small:
        copy.wait()
    prepare(x)
    gcen[...] = jnp.zeros_like(gcen)
    gcoef[...] = jnp.zeros_like(gcoef)
    tot[...] = jnp.zeros_like(tot)

    def wide(col):
        return jnp.concatenate([col] * (CORES * q // 128), axis=1)

    def cols_of(xi):
        return pl.ds(pl.multiple_of(xi * CORES * q, CORES * q), CORES * q)

    def rows_of(b, xi):
        return pts[b, pl.ds(xi * CORES, CORES)].reshape(CORES * q, width).T

    def put_pred(b, total):
        for co in range(CORES):
            pred[b, co] = total[:, co * q:(co + 1) * q]

    def square_sum(rows_t):
        r32 = rows_t.astype(f32)
        return jnp.sum(r32 * r32, axis=0, keepdims=True)

    def kernel_of(rows_t, psq, xi):
        cross = jnp.dot(cm2[xi], rows_t, preferred_element_type=f32)
        dist = (psq + wide(csq[xi])) + cross
        return jnp.exp2(wide(nrate[xi]) * dist).astype(bf16)

    def forward_own(b):
        rows_t = rows_of(b, x)
        psq = square_sum(rows_t)
        ptst[b] = rows_t
        psqs[b] = psq
        k = kernel_of(rows_t, psq, x)
        kt[b, :, cols_of(x)] = k
        put_pred(b, jnp.dot(coeft[x], k, preferred_element_type=f32))

    def forward_rest(b):
        rows_t, psq = ptst[b], psqs[b]
        total = jnp.concatenate([pred[b, co] for co in range(CORES)], axis=1)
        for i in range(1, X):
            k = kernel_of(rows_t, psq, off[i])
            total = total + jnp.dot(coeft[off[i]], k, preferred_element_type=f32)
        put_pred(b, total)
        pccopy(b).start()

    def kernel_rest(b):
        for i in range(1, X):
            rows_t = rows_of(b, back[i])
            kt[b, :, cols_of(back[i])] = kernel_of(rows_t, square_sum(rows_t), x)

    def backward(b):
        for t in range(C):
            cols = slice(t * q, (t + 1) * q)
            mix = lax.dot_general(coef[x], cot[b, t], (((1,), (1,)), ((), ())),
                                  preferred_element_type=f32)
            w = (kt[b, :, cols].astype(f32) * mix).astype(bf16)
            w32 = w.astype(f32)
            part = w32[:, :128]
            for i in range(1, q // 128):
                part = part + w32[:, i * 128:(i + 1) * 128]
            tot[...] += part
            wbuf[:, cols] = w
        gcen[...] += jnp.dot(wbuf[...], pts[b].reshape(C * q, width), preferred_element_type=f32)
        gcoef[...] += jnp.dot(kt[b], cot[b].reshape(C * q, cot.shape[3]),
                              preferred_element_type=f32)

    def arrive(b, s):
        zcopy(0, b, s).wait_recv()

        @pl.when((b < z) & (z + 1 < Z))
        def _():
            zcopy(0, b, s).start()

        @pl.when((b > z) & (z > 0))
        def _():
            zcopy(1, b, s).start()
        ccopy(b, x, s).start()

    def arrivals(d):
        for s in range(SUBS):
            blocks(d, lambda b: arrive(b, s))

    def send_x(b):
        for s in range(SUBS):
            for k in range(1, X):
                xcopy(b, k, s).start()

    def own_lanes(b):
        for s in range(SUBS):
            ccopy(b, x, s, coming=True).wait_recv()

    def work(b):
        own_lanes(b)
        forward_own(b)

    def forward_all(b):
        own_lanes(b)
        rows_t = rows_of(b, x)
        psq = square_sum(rows_t)
        k = kernel_of(rows_t, psq, x)
        kt[b, :, cols_of(x)] = k
        total = jnp.dot(coeft[x], k, preferred_element_type=f32)
        for i in range(1, X):
            k = kernel_of(rows_t, psq, off[i])
            total = total + jnp.dot(coeft[off[i]], k, preferred_element_type=f32)
        put_pred(b, total)
        pccopy(b).start()

    def finish(b):
        pccopy(b).wait_recv()
        psum[b] = pred[b, core] + pc[b]

        @pl.when(b != z)
        def _():
            pzcopy(b, z).start()

    def rest(b):
        for s in range(SUBS):
            for k in range(1, X):
                xcopy(b, k, s, coming=True).wait_recv()
                ccopy(b, back[k], s).start()
        for s in range(SUBS):
            for k in range(1, X):
                ccopy(b, back[k], s, coming=True).wait_recv()
        kernel_rest(b)

    own_points.wait()
    forward_own(z)
    kernel_rest(z)

    def early(d, carry):
        arrivals(d)
        blocks(d, work)
        return carry
    lax.fori_loop(1, Z - 1, early, 0)

    for k in range(1, X):
        for copy in ecopies(k, coming=True):
            copy.wait_recv()
        prepare(back[k])

    def middle(d, carry):
        blocks(d, send_x)
        blocks(d, forward_rest, 0)
        blocks(d - 1, finish, 0)
        return carry
    lax.fori_loop(0, Z - 1, middle, 0)
    blocks(Z - 2, finish, 0)
    arrivals(Z - 1)
    blocks(Z - 1, send_x)
    blocks(Z - 1, forward_all)
    blocks(Z - 1, finish)

    total = psum[z]
    for k in range(1, Z):
        src = lax.rem(z + k, Z)
        pzcopy(src, src).wait_recv()
        total = total + pz[src]
    own_saved.wait()
    own_target.wait()
    residual = total.T + sv[...] - tg[...]
    ratio = residual / delta[...]
    cot[z, c] = (residual / jnp.sqrt(1.0 + ratio * ratio)).astype(bf16)
    for k in range(1, Z):
        czcopy(z, lax.rem(z + k, Z)).start()

    def spread_cot(b):
        for k in range(1, X):
            cxcopy(b, k).start()
        cccopy(b, x).start()

    def cot_arrive(b):
        czcopy(b, b).wait_recv()
        spread_cot(b)

    def cot_cross(b):
        for k in range(1, X):
            cxcopy(b, k, coming=True).wait_recv()
            cccopy(b, back[k]).start()

    def cot_work(b):
        for xi in range(X):
            cccopy(b, xi, coming=True).wait_recv()
        backward(b)

    spread_cot(z)

    blocks(1, rest)
    blocks(1, cot_arrive)
    blocks(2, rest)
    cot_cross(z)
    cot_work(z)

    def late(d, carry):
        blocks(d - 1, cot_arrive)
        blocks(d, rest)
        return carry
    lax.fori_loop(3, Z + 1, late, 0)
    blocks(1, cot_cross)

    def last(d, carry):
        blocks(d + 1, cot_cross)
        blocks(d, cot_work)
        return carry
    lax.fori_loop(1, Z, last, 0)

    row_totals = jnp.sum(tot[...], axis=1, keepdims=True)
    scale = (-2.0 / LOG2E) * nrate[x]
    scale = jnp.concatenate([scale] * (width // 128), axis=1)
    gcen[...] = scale * (gcen[...] - row_totals * cen[x].astype(f32))

    def drain(b, carry):
        for s in range(SUBS):
            @pl.when((b <= z) & (z + 1 < Z))
            def _():
                zcopy(0, b, s).wait_send()

            @pl.when((b >= z) & (z > 0))
            def _():
                zcopy(1, b, s).wait_send()

        @pl.when(b != z)
        def _():
            for s in range(SUBS):
                for k in range(1, X):
                    xcopy(b, k, s).wait_send()
                for xi in range(X):
                    ccopy(b, xi, s).wait_send()
            pzcopy(b, z).wait_send()
            czcopy(z, b).wait_send()
        pccopy(b).wait_send()
        for k in range(1, X):
            cxcopy(b, k).wait_send()
        for xi in range(X):
            cccopy(b, xi).wait_send()
        return carry
    lax.fori_loop(0, Z, drain, 0)
    for k in range(1, X):
        for copy in ecopies(k):
            copy.wait_send()


def per_device(Z, C, train_points, saved_preds, targets, huber_delta, center_pos, coefficients, spread):
    n_points, width = train_points.shape
    n_cen, n_out = coefficients.shape
    X, q = C // CORES, n_points // C
    vm, in_hbm = pl.BlockSpec(memory_space=pltpu.VMEM), pl.BlockSpec(memory_space=pltpu.HBM)
    dma = pltpu.SemaphoreType.DMA
    flops = 2 * Z * n_points * n_cen * (2 * width + 3 * n_out)
    return tuple(pl.pallas_call(
        functools.partial(body, Z, C),
        out_shape=(pltpu.VMEM((n_cen, width), f32), pltpu.VMEM((n_cen, n_out), f32)),
        in_specs=[in_hbm] * 7,
        out_specs=(vm, vm),
        scratch_shapes=[
            pltpu.VMEM((Z, C, q, width), bf16),
            pltpu.VMEM((Z, width, CORES * q), bf16),
            pltpu.VMEM((Z, 1, CORES * q), f32),
            pltpu.VMEM((Z, n_cen, C * q), bf16),
            pltpu.VMEM((Z, CORES, n_out, q), f32),
            pltpu.VMEM((Z, n_out, q), f32),
            pltpu.VMEM((Z, n_out, q), f32),
            pltpu.VMEM((Z, n_out, q), f32),
            pltpu.VMEM((Z, C, q, n_out), bf16),
            pltpu.VMEM((X, n_cen, width), bf16),
            pltpu.VMEM((X, n_out, n_cen), bf16),
            pltpu.VMEM((X, n_cen, 128), f32),
            pltpu.VMEM((X, n_cen, 128), f32),
            pltpu.VMEM((n_cen, 128), f32),
            pltpu.VMEM((n_cen, C * q), bf16),
            pltpu.VMEM((q, n_out), f32),
            pltpu.VMEM((q, n_out), f32),
            pltpu.VMEM((1, n_out), f32),
            pltpu.VMEM((X, 1, n_cen), f32),
            pltpu.VMEM((X, n_cen, width), bf16),
            pltpu.VMEM((X, n_cen, n_out), bf16),
            dma((2, Z, SUBS)), dma((Z, SUBS)),
            dma((Z, X, SUBS)), dma((Z, X, SUBS)),
            dma((Z, X, SUBS)), dma((Z, X, SUBS)),
            dma((Z,)), dma((Z,)),
            dma((Z,)), dma((Z,)),
            dma((Z,)), dma((Z,)),
            dma((Z, X)), dma((Z, X)),
            dma((Z, X)), dma((Z, X)),
            dma((X, 3)), dma((X, 3)),
            dma((7,)),
        ],
        compiler_params=pltpu.CompilerParams(
            collective_id=0, has_side_effects=True, vmem_limit_bytes=60 << 20),
        cost_estimate=pl.CostEstimate(
            flops=flops, bytes_accessed=4 << 20, transcendentals=Z * n_points * n_cen),
    )(train_points.reshape(C, q, width), saved_preds.reshape(C, q, n_out),
      targets.reshape(C, q, n_out), huber_delta.reshape(1, n_out),
      spread.astype(f32).reshape(1, n_cen), center_pos, coefficients))


def solution(mesh):
    rows = P(("groups", "points"), None)
    owned = P(("groups", "points", "centers"), None)
    return jax.shard_map(
        functools.partial(per_device, mesh.shape["points"], mesh.shape["centers"]),
        mesh=mesh,
        in_specs=(rows, rows, rows, P("groups"), owned, owned, P(("groups", "points", "centers"))),
        out_specs=(owned, owned),
        check_vma=False,
    )
```

```python
import functools

import jax
import jax.numpy as jnp
from jax import lax
from jax.experimental import pallas as pl
from jax.experimental.pallas import tpu as pltpu
from jax.sharding import PartitionSpec as P

CORES = 2
SUBS = 2
LOG2E = 1.4426950408889634
MESH = pl.DeviceIdType.MESH
f32, bf16 = jnp.float32, jnp.bfloat16


def body(Z, C, train, saved, target, delta_in, rates_in, cen_in, coef_in, gcen, gcoef,
         pts, ptst, psqs, kt, pred, pc, psum, pz, cot, cm2, coeft, csq, nrate, tot, wbuf, sv, tg,
         delta, rates, cen, coef,
         zs, zr, xs, xr, cs, cr, pcs, pcr, pzs, pzr,
         czs, czr, cxs, cxr, ccs, ccr, es, er, ls):
    X = C // CORES
    q, width = pts.shape[2], pts.shape[3]
    sub = q // SUBS
    z, c = lax.axis_index("points"), lax.axis_index("centers")
    x, core = lax.div(c, CORES), lax.rem(c, CORES)
    other = 1 - core
    mate = x * CORES + other
    off = [lax.rem(x + k, X) for k in range(X)]
    back = [lax.rem(x + X - k, X) for k in range(X)]

    def remote(src, dst, ssem, rsem, **to):
        return pltpu.make_async_remote_copy(
            src_ref=src, dst_ref=dst, send_sem=ssem, recv_sem=rsem, device_id=to,
            device_id_type=MESH)

    def lane(xi, co):
        return xi * CORES + co

    def zcopy(way, b, s, own=False):
        rows = pl.ds(s * sub, sub)
        dst = pts.at[b, c, rows]
        src = train.at[c, rows] if own else dst
        to = z + 1 if way == 0 else z - 1
        return remote(src, dst, zs.at[way, b, s], zr.at[b, s], points=to)

    def xcopy(b, k, s, coming=False):
        li = lane(back[k], core) if coming else c
        ref = pts.at[b, li, pl.ds(s * sub, sub)]
        return remote(ref, ref, xs.at[b, k, s], xr.at[b, k, s], centers=lane(off[k], core))

    def ccopy(b, xi, s, coming=False):
        ref = pts.at[b, lane(xi, other if coming else core), pl.ds(s * sub, sub)]
        return remote(ref, ref, cs.at[b, xi, s], cr.at[b, xi, s], centers=mate)

    def ecopies(k, coming=False):
        at = back[k] if coming else x
        return [remote(src, dst.at[at], es.at[k, i], er.at[k, i], centers=lane(off[k], core))
                for i, (src, dst) in enumerate(
                    ((cen_in, cen), (coef_in, coef), (rates.at[x], rates)))]

    def pccopy(b):
        return remote(pred.at[b, other], pc.at[b], pcs.at[b], pcr.at[b], centers=mate)

    def pzcopy(b, src_z):
        return remote(psum.at[b], pz.at[src_z], pzs.at[b], pzr.at[src_z], points=b)

    def czcopy(b, to):
        ref = cot.at[b, c]
        return remote(ref, ref, czs.at[to], czr.at[b], points=to)

    def cxcopy(b, k, coming=False):
        ref = cot.at[b, lane(back[k], core) if coming else c]
        return remote(ref, ref, cxs.at[b, k], cxr.at[b, k], centers=lane(off[k], core))

    def cccopy(b, xi, coming=False):
        ref = cot.at[b, lane(xi, other if coming else core)]
        return remote(ref, ref, ccs.at[b, xi], ccr.at[b, xi], centers=mate)

    def blocks(d, f, first=1):
        @pl.when((d >= first) & (d < Z) & (z - d >= 0))
        def _():
            f(z - d)

        @pl.when((d >= max(first, 1)) & (d < Z) & (z + d < Z))
        def _():
            f(z + d)

    barrier = pltpu.get_barrier_semaphore()
    for k in range(1, Z):
        pl.semaphore_signal(barrier, inc=1, device_id={"points": lax.rem(z + k, Z)},
                            device_id_type=MESH)
    for k in range(1, X):
        pl.semaphore_signal(barrier, inc=1, device_id={"centers": lane(off[k], core)},
                            device_id_type=MESH)
    pl.semaphore_signal(barrier, inc=1, device_id={"centers": mate}, device_id_type=MESH)
    own_points = pltpu.make_async_copy(train, pts.at[z], ls.at[0])
    own_saved = pltpu.make_async_copy(saved.at[c], sv, ls.at[1])
    own_target = pltpu.make_async_copy(target.at[c], tg, ls.at[2])
    own_points.start()
    own_saved.start()
    own_target.start()
    rates[x] = rates_in[...].astype(f32).reshape(1, rates.shape[2])
    small = [pltpu.make_async_copy(a, b, ls.at[3 + i]) for i, (a, b) in enumerate(
        ((cen_in, cen.at[x]), (coef_in, coef.at[x]), (delta_in, delta)))]
    for copy in small:
        copy.start()
    pl.semaphore_wait(barrier, Z - 1 + X - 1 + 1)

    for s in range(SUBS):
        @pl.when(z + 1 < Z)
        def _():
            zcopy(0, z, s, own=True).start()

        @pl.when(z > 0)
        def _():
            zcopy(1, z, s, own=True).start()

    for k in range(1, X):
        for copy in ecopies(k):
            copy.start()

    n_cen = cen.shape[1]

    def prepare(xi):
        cen32 = cen[xi].astype(f32)
        cm2[xi] = (-2.0 * cen32).astype(bf16)
        coeft[xi] = coef[xi].astype(f32).T.astype(bf16)
        csq[xi] = jnp.broadcast_to(jnp.sum(cen32 * cen32, axis=1, keepdims=True), (n_cen, 128))
        nrate[xi] = jnp.broadcast_to(rates[xi] * (-LOG2E / width), (128, n_cen)).T

    for copy in small:
        copy.wait()
    prepare(x)
    gcen[...] = jnp.zeros_like(gcen)
    gcoef[...] = jnp.zeros_like(gcoef)
    tot[...] = jnp.zeros_like(tot)

    def wide(col):
        return jnp.concatenate([col] * (CORES * q // 128), axis=1)

    def cols_of(xi):
        return pl.ds(pl.multiple_of(xi * CORES * q, CORES * q), CORES * q)

    def rows_of(b, xi):
        return pts[b, pl.ds(xi * CORES, CORES)].reshape(CORES * q, width).T

    def put_pred(b, total):
        for co in range(CORES):
            pred[b, co] = total[:, co * q:(co + 1) * q]

    def square_sum(rows_t):
        r32 = rows_t.astype(f32)
        return jnp.sum(r32 * r32, axis=0, keepdims=True)

    def kernel_of(rows_t, psq, xi):
        cross = jnp.dot(cm2[xi], rows_t, preferred_element_type=f32)
        dist = (psq + wide(csq[xi])) + cross
        return jnp.exp2(wide(nrate[xi]) * dist).astype(bf16)

    def forward_own(b):
        rows_t = rows_of(b, x)
        psq = square_sum(rows_t)
        ptst[b] = rows_t
        psqs[b] = psq
        k = kernel_of(rows_t, psq, x)
        kt[b, :, cols_of(x)] = k
        put_pred(b, jnp.dot(coeft[x], k, preferred_element_type=f32))

    def forward_rest(b):
        rows_t, psq = ptst[b], psqs[b]
        total = jnp.concatenate([pred[b, co] for co in range(CORES)], axis=1)
        for i in range(1, X):
            k = kernel_of(rows_t, psq, off[i])
            total = total + jnp.dot(coeft[off[i]], k, preferred_element_type=f32)
        put_pred(b, total)
        pccopy(b).start()

    def kernel_rest(b):
        for i in range(1, X):
            rows_t = rows_of(b, back[i])
            kt[b, :, cols_of(back[i])] = kernel_of(rows_t, square_sum(rows_t), x)

    def backward(b):
        for t in range(C):
            cols = slice(t * q, (t + 1) * q)
            mix = lax.dot_general(coef[x], cot[b, t], (((1,), (1,)), ((), ())),
                                  preferred_element_type=f32)
            w = (kt[b, :, cols].astype(f32) * mix).astype(bf16)
            w32 = w.astype(f32)
            part = w32[:, :128]
            for i in range(1, q // 128):
                part = part + w32[:, i * 128:(i + 1) * 128]
            tot[...] += part
            wbuf[:, cols] = w
        gcen[...] += jnp.dot(wbuf[...], pts[b].reshape(C * q, width), preferred_element_type=f32)
        gcoef[...] += jnp.dot(kt[b], cot[b].reshape(C * q, cot.shape[3]),
                              preferred_element_type=f32)

    def arrive(b, s):
        zcopy(0, b, s).wait_recv()

        @pl.when((b < z) & (z + 1 < Z))
        def _():
            zcopy(0, b, s).start()

        @pl.when((b > z) & (z > 0))
        def _():
            zcopy(1, b, s).start()
        ccopy(b, x, s).start()

    def arrivals(d):
        for s in range(SUBS):
            blocks(d, lambda b: arrive(b, s))

    def send_x(b):
        for s in range(SUBS):
            for k in range(1, X):
                xcopy(b, k, s).start()

    def own_lanes(b):
        for s in range(SUBS):
            ccopy(b, x, s, coming=True).wait_recv()

    def work(b):
        own_lanes(b)
        forward_own(b)

    def forward_all(b):
        own_lanes(b)
        rows_t = rows_of(b, x)
        psq = square_sum(rows_t)
        k = kernel_of(rows_t, psq, x)
        kt[b, :, cols_of(x)] = k
        total = jnp.dot(coeft[x], k, preferred_element_type=f32)
        for i in range(1, X):
            k = kernel_of(rows_t, psq, off[i])
            total = total + jnp.dot(coeft[off[i]], k, preferred_element_type=f32)
        put_pred(b, total)
        pccopy(b).start()

    def finish(b):
        pccopy(b).wait_recv()
        psum[b] = pred[b, core] + pc[b]

        @pl.when(b != z)
        def _():
            pzcopy(b, z).start()

    def rest(b):
        for s in range(SUBS):
            for k in range(1, X):
                xcopy(b, k, s, coming=True).wait_recv()
                ccopy(b, back[k], s).start()
        for s in range(SUBS):
            for k in range(1, X):
                ccopy(b, back[k], s, coming=True).wait_recv()
        kernel_rest(b)

    own_points.wait()
    forward_own(z)
    kernel_rest(z)

    def early(d, carry):
        arrivals(d)
        blocks(d, work)
        return carry
    lax.fori_loop(1, Z - 1, early, 0)

    for k in range(1, X):
        for copy in ecopies(k, coming=True):
            copy.wait_recv()
        prepare(back[k])

    def middle(d, carry):
        blocks(d, send_x)
        blocks(d, forward_rest, 0)
        blocks(d - 1, finish, 0)
        return carry
    lax.fori_loop(0, Z - 1, middle, 0)
    blocks(Z - 2, finish, 0)
    arrivals(Z - 1)
    blocks(Z - 1, send_x)
    blocks(Z - 1, forward_all)
    blocks(Z - 1, finish)

    total = psum[z]
    for k in range(1, Z):
        src = lax.rem(z + k, Z)
        pzcopy(src, src).wait_recv()
        total = total + pz[src]
    own_saved.wait()
    own_target.wait()
    residual = total.T + sv[...] - tg[...]
    ratio = residual / delta[...]
    cot[z, c] = (residual / jnp.sqrt(1.0 + ratio * ratio)).astype(bf16)
    for k in range(1, Z):
        czcopy(z, lax.rem(z + k, Z)).start()

    def spread_cot(b):
        for k in range(1, X):
            cxcopy(b, k).start()
        cccopy(b, x).start()

    def cot_arrive(b):
        czcopy(b, b).wait_recv()
        spread_cot(b)

    def cot_cross(b):
        for k in range(1, X):
            cxcopy(b, k, coming=True).wait_recv()
            cccopy(b, back[k]).start()

    def cot_work(b):
        for xi in range(X):
            cccopy(b, xi, coming=True).wait_recv()
        backward(b)

    spread_cot(z)

    blocks(1, rest)
    blocks(1, cot_arrive)
    blocks(2, rest)
    cot_cross(z)
    cot_work(z)

    def late(d, carry):
        blocks(d - 1, cot_arrive)
        blocks(d, rest)
        return carry
    lax.fori_loop(3, Z + 1, late, 0)
    blocks(1, cot_cross)

    def last(d, carry):
        blocks(d + 1, cot_cross)
        blocks(d, cot_work)
        return carry
    lax.fori_loop(1, Z, last, 0)

    row_totals = jnp.sum(tot[...], axis=1, keepdims=True)
    scale = (-2.0 / LOG2E) * nrate[x]
    scale = jnp.concatenate([scale] * (width // 128), axis=1)
    gcen[...] = scale * (gcen[...] - row_totals * cen[x].astype(f32))

    def drain(b, carry):
        for s in range(SUBS):
            @pl.when((b <= z) & (z + 1 < Z))
            def _():
                zcopy(0, b, s).wait_send()

            @pl.when((b >= z) & (z > 0))
            def _():
                zcopy(1, b, s).wait_send()

        @pl.when(b != z)
        def _():
            for s in range(SUBS):
                for k in range(1, X):
                    xcopy(b, k, s).wait_send()
                for xi in range(X):
                    ccopy(b, xi, s).wait_send()
            pzcopy(b, z).wait_send()
            czcopy(z, b).wait_send()
        pccopy(b).wait_send()
        for k in range(1, X):
            cxcopy(b, k).wait_send()
        for xi in range(X):
            cccopy(b, xi).wait_send()
        return carry
    lax.fori_loop(0, Z, drain, 0)
    for k in range(1, X):
        for copy in ecopies(k):
            copy.wait_send()


def per_device(Z, C, train_points, saved_preds, targets, huber_delta, center_pos, coefficients, spread):
    n_points, width = train_points.shape
    n_cen, n_out = coefficients.shape
    X, q = C // CORES, n_points // C
    vm, in_hbm = pl.BlockSpec(memory_space=pltpu.VMEM), pl.BlockSpec(memory_space=pltpu.HBM)
    dma = pltpu.SemaphoreType.DMA
    flops = 2 * Z * n_points * n_cen * (2 * width + 3 * n_out)
    return tuple(pl.pallas_call(
        functools.partial(body, Z, C),
        out_shape=(pltpu.VMEM((n_cen, width), f32), pltpu.VMEM((n_cen, n_out), f32)),
        in_specs=[in_hbm] * 4 + [vm] + [in_hbm] * 2,
        out_specs=(vm, vm),
        scratch_shapes=[
            pltpu.VMEM((Z, C, q, width), bf16),
            pltpu.VMEM((Z, width, CORES * q), bf16),
            pltpu.VMEM((Z, 1, CORES * q), f32),
            pltpu.VMEM((Z, n_cen, C * q), bf16),
            pltpu.VMEM((Z, CORES, n_out, q), f32),
            pltpu.VMEM((Z, n_out, q), f32),
            pltpu.VMEM((Z, n_out, q), f32),
            pltpu.VMEM((Z, n_out, q), f32),
            pltpu.VMEM((Z, C, q, n_out), bf16),
            pltpu.VMEM((X, n_cen, width), bf16),
            pltpu.VMEM((X, n_out, n_cen), bf16),
            pltpu.VMEM((X, n_cen, 128), f32),
            pltpu.VMEM((X, n_cen, 128), f32),
            pltpu.VMEM((n_cen, 128), f32),
            pltpu.VMEM((n_cen, C * q), bf16),
            pltpu.VMEM((q, n_out), f32),
            pltpu.VMEM((q, n_out), f32),
            pltpu.VMEM((1, n_out), f32),
            pltpu.VMEM((X, 1, n_cen), f32),
            pltpu.VMEM((X, n_cen, width), bf16),
            pltpu.VMEM((X, n_cen, n_out), bf16),
            dma((2, Z, SUBS)), dma((Z, SUBS)),
            dma((Z, X, SUBS)), dma((Z, X, SUBS)),
            dma((Z, X, SUBS)), dma((Z, X, SUBS)),
            dma((Z,)), dma((Z,)),
            dma((Z,)), dma((Z,)),
            dma((Z,)), dma((Z,)),
            dma((Z, X)), dma((Z, X)),
            dma((Z, X)), dma((Z, X)),
            dma((X, 3)), dma((X, 3)),
            dma((7,)),
        ],
        compiler_params=pltpu.CompilerParams(
            collective_id=0, has_side_effects=True, vmem_limit_bytes=60 << 20),
        cost_estimate=pl.CostEstimate(
            flops=flops, bytes_accessed=4 << 20, transcendentals=Z * n_points * n_cen),
    )(train_points.reshape(C, q, width), saved_preds.reshape(C, q, n_out),
      targets.reshape(C, q, n_out), huber_delta.reshape(1, n_out),
      spread, center_pos, coefficients))


def solution(mesh):
    rows = P(("groups", "points"), None)
    owned = P(("groups", "points", "centers"), None)
    return jax.shard_map(
        functools.partial(per_device, mesh.shape["points"], mesh.shape["centers"]),
        mesh=mesh,
        in_specs=(rows, rows, rows, P("groups"), owned, owned, P(("groups", "points", "centers"))),
        out_specs=(owned, owned),
        check_vma=False,
    )
```
